512 devices in a mesh: dp: 16 (over y_lo, x), expert: 32 (over z, y_hi, core).
Axes of the slice: x: 4, y: 8 (y_hi: 2, y_lo: 4; y = y_hi * 4 + y_lo), z: 8, core: 2. Of those that a mesh axis runs over, the one named last changes fastest.
Arguments:
- tokens: bfloat16 [6144, 4096], P('expert', 'dp'), may hold values from -6 to 6
- cotangent: bfloat16 [6144, 4096], P('expert', 'dp'), may hold values from -4 to 4
- expert_ids: int32 [6144, 2], P('expert'), may hold values from 0 to 31, all different within a row; in each aligned block of 192 rows (0 to 191, 192 to 383, ...) at most 24 rows name the same one
- gate_values: float32 [6144, 2], P('expert'), may hold values from 0.1 to 0.9
- gate_up_weight: bfloat16 [32, 4096, 2048], P('expert', 'dp'), may hold values from -0.09375 to 0.09375
- down_weight: bfloat16 [32, 1024, 4096], P('expert', None, 'dp'), may hold values from -0.1875 to 0.1875
Outputs:
- layer_output: bfloat16 [6144, 4096], P('expert', 'dp')
- token_gradient: bfloat16 [6144, 4096], P('expert', 'dp')
- gate_gradient: float32 [6144, 2], P('expert')
- gate_up_gradient: bfloat16 [32, 4096, 2048], P('expert', 'dp')
- down_gradient: bfloat16 [32, 1024, 4096], P('expert', None, 'dp')
The draws below stay inside these ranges and needn't reach their ends.
Inputs may be any that keep to these rules, and one draw needn't show every extreme that they name: `expert_ids`: each token names two different experts. In each aligned block of 192 tokens no expert is named more than 24 times, a bound that some block reaches.
All inputs are finite; a program needn't handle non-finite values. Where the reference program divides by a largest or mean magnitude, that divisor is 1e-20 or more.
Results may differ from the reference program's by a relative error of at most 0.04.
Values may be sent and summed in bfloat16 or wider, within the bound.
A program may use at most 64 MiB of HBM per device.

```python
import math
import jax
import jax.numpy as jnp
import numpy as np
from jax import lax

D = 4096
FF = 1024
HB = 128
TOK_DEV = 192
EXPERTS = 32
CAP = 24
TOKENS = 6144
N_DP = 16
N_EXPERT = 32


def level_of(key, extent, split, least, top_value):
    factor_of = 1.0
    for position, blocks in split:
        draws = jax.random.uniform(jax.random.fold_in(jax.random.fold_in(key, 6), position), (blocks,), jnp.float32, least / len(split), top_value / len(split))
        factor_of = factor_of * jnp.repeat(jnp.exp(draws), extent[position] // blocks).reshape((-1,) + (1,) * (len(extent) - 1 - position))
    return factor_of


def assign_block(rng, own, number, rows, number_of, top, reach, lean):
    sequence = jax.random.permutation(rng, number_of)
    heavy_load, usual = load_shares(number_of, rows * top, reach, lean, True), load_shares(number_of, rows * top, reach, lean, False)
    places = jnp.arange(number_of)

    def named(sizes, rotation):
        used = int((sizes > 0).sum())
        fixed = max(1, used // 4)
        passed = fixed + (places - fixed + rotation * (used - fixed)) % max(1, number_of - fixed)
        return jnp.zeros((number_of,), jnp.int32).at[sequence[jnp.where(places < fixed, places, passed)]].set(jnp.asarray(sizes, jnp.int32))

    sizes = jnp.where(number % 4 == 0, named(heavy_load, number // 4), named(usual, number - number // 4 - 1))
    mixed = jax.random.permutation(jax.random.fold_in(own, 3), number_of)
    giver, taker = mixed[0:number_of // 2 * 2:2], mixed[1:number_of // 2 * 2:2]
    slack = jnp.minimum(sizes[giver] - 1, reach - sizes[taker]) // 2
    slack = jnp.where((giver == sequence[0]) | (taker == sequence[0]) | (sizes[taker] == 0), 0, jnp.maximum(slack, 0))
    passed = jax.random.randint(jax.random.fold_in(own, 4), (number_of // 2,), 0, 1 << 20) % (slack + 1)
    sizes = sizes.at[giver].add(-passed).at[taker].add(passed)
    members = jnp.searchsorted(jnp.cumsum(sizes), jnp.arange(rows * top), side="right").astype(jnp.int32)
    grid = members.reshape(top, rows).T
    grid = grid[jax.random.permutation(jax.random.fold_in(own, 1), rows)]
    rotation = jax.random.randint(jax.random.fold_in(own, 2), (rows, 1), 0, top)
    return jnp.take_along_axis(grid, (jnp.arange(top)[None, :] + rotation) % top, axis=1)


def load_shares(count, total, limit, lean, full):
    loads = [(1 << 20) // math.isqrt(rank ** lean) + 1 for rank in range(1, count + 1)]
    largest = limit if full else min(limit, max(-(-total // count), total * loads[0] // sum(loads)))
    least = 1 if total - largest >= count - 1 else 0
    counts, rest = [largest] + [least] * (count - 1), total - largest - least * (count - 1)
    while rest > 0:
        movable = [i for i in range(1, count) if counts[i] < largest] or [i for i in range(1, count) if counts[i] < limit]
        whole, left = sum([loads[i] for i in movable]), rest
        for i in movable:
            more = min(limit - counts[i], max(1, left * loads[i] // whole), rest)
            counts[i] = counts[i] + more
            rest = rest - more
    return np.array(counts)


def bell_draw(own_key, shape, deviation, limit, cuts=(), kind=jnp.bfloat16):
    entries = deviation * jax.random.normal(own_key, shape, jnp.float32)
    if cuts:
        entries = entries * level_of(own_key, shape, cuts, -0.22, 0.18)
    return jnp.clip(entries, -limit, limit).astype(kind)


def setup_inputs(seed: int = 0) -> dict:
    seeds = jax.random.split(jax.random.key(seed), 7)
    tokens = bell_draw(seeds[0], (TOKENS, D), 1.0, 6.0, ((0, 32), (1, 16)))
    cotangent = bell_draw(seeds[1], (TOKENS, D), 0.25, 4.0, ((0, 32), (1, 16)))
    expert_ids_keys = jax.random.split(jax.random.fold_in(seeds[2], 1), TOKENS // TOK_DEV)
    expert_ids_turns = jax.random.permutation(jax.random.fold_in(seeds[2], 3), TOKENS // TOK_DEV)
    expert_ids = jax.vmap(lambda own, number: assign_block(jax.random.fold_in(seeds[2], 2), own, number, TOK_DEV, EXPERTS, 2, CAP, 2))(expert_ids_keys, expert_ids_turns).reshape((TOKENS, 2))
    gate_values = jnp.clip(0.1 + 0.79999997 * jax.random.uniform(seeds[3], (TOKENS, 2), jnp.float32) ** level_of(seeds[3], (TOKENS, 2), ((0, 32),), -0.2, 0.2), 0.1, 0.9)
    gate_up_weight = bell_draw(seeds[4], (EXPERTS, D, 2 * FF), D ** -0.5, 0.09375, ((0, 32), (1, 16)))
    down_weight = bell_draw(seeds[5], (EXPERTS, FF, D), FF ** -0.5, 0.1875, ((0, 32), (2, 16)))
    return {"tokens": tokens, "cotangent": cotangent, "expert_ids": expert_ids, "gate_values": gate_values, "gate_up_weight": gate_up_weight, "down_weight": down_weight}


def hadamard_signs(table_order):
    row_bits = jnp.arange(table_order, dtype=jnp.int32)[:, None]
    col_bits = jnp.arange(table_order, dtype=jnp.int32)[None, :]
    parity = jnp.zeros((table_order, table_order), jnp.int32)
    for bit_index in range(table_order.bit_length() - 1):
        common_bits = jnp.bitwise_and(jnp.right_shift(row_bits, bit_index), jnp.right_shift(col_bits, bit_index))
        parity = parity + jnp.bitwise_and(common_bits, 1)
    return (1 - 2 * jnp.bitwise_and(parity, 1)).astype(jnp.float32)


def rotate_blocks(values, sign_table):
    count_rows, features = values.shape
    blocks = values.astype(jnp.float32).reshape(count_rows, features // HB, HB)
    turned = jnp.einsum("nbi,ij->nbj", blocks, sign_table, precision=lax.Precision.HIGHEST) * (HB ** -0.5)
    return turned.reshape(count_rows, features)


def quantize(turned):
    count_rows, features = turned.shape
    blocks = turned.reshape(count_rows, features // HB, HB)
    block_scale = (jnp.max(jnp.abs(blocks), axis=2) + 1e-6).astype(jnp.bfloat16)
    coded_rows = (blocks / block_scale.astype(jnp.float32)[:, :, None]).astype(jnp.bfloat16)
    return coded_rows.reshape(count_rows, features), block_scale


def restore(coded_rows, block_scale):
    count_rows, features = coded_rows.shape
    blocks = coded_rows.astype(jnp.float32).reshape(count_rows, features // HB, HB)
    restored = (blocks * block_scale.astype(jnp.float32)[:, :, None]).astype(jnp.bfloat16)
    return restored.reshape(count_rows, features)


def slot_positions(block_ids, experts):
    flat_ids = block_ids.reshape(-1)
    onehot = (flat_ids[:, None] == jnp.arange(experts, dtype=jnp.int32)[None, :]).astype(jnp.int32)
    earlier = jnp.cumsum(onehot, axis=0) - onehot
    return jnp.sum(onehot * earlier, axis=1).astype(jnp.int32).reshape(block_ids.shape)


def unrotate_pairs(picked, sign_table):
    count_rows, pair_count, features = picked.shape
    blocks = picked.astype(jnp.float32).reshape(count_rows, pair_count, features // HB, HB)
    turned = jnp.einsum("nkbi,ij->nkbj", blocks, sign_table, precision=lax.Precision.HIGHEST) * (HB ** -0.5)
    return jnp.sum(turned, axis=1).reshape(count_rows, features)


def sliced_sum(left_side, right_side, einsum_form):
    partials = jnp.einsum(einsum_form, left_side.astype(jnp.float32), right_side.astype(jnp.float32), precision=lax.Precision.HIGHEST)
    rounded = lax.optimization_barrier(partials.astype(jnp.bfloat16))
    return jnp.sum(rounded.astype(jnp.float32), axis=0)


def expert_pass(operands):
    restored, expert_grad, gate_up, down_matrix = operands
    count_rows = restored.shape[0]
    width_slice = D // N_DP
    pre_act = sliced_sum(restored.reshape(count_rows, N_DP, width_slice), gate_up.reshape(N_DP, width_slice, 2 * FF), "rsk,skf->srf")
    gate_pre = pre_act[:, :FF]
    up_pre = pre_act[:, FF:]
    sigmoid_gate = jax.nn.sigmoid(gate_pre)
    activated = gate_pre * sigmoid_gate
    hidden = (activated * up_pre).astype(jnp.bfloat16)
    expert_out = jnp.dot(hidden, down_matrix, preferred_element_type=jnp.float32).astype(jnp.bfloat16)
    down_gradient = lax.dot_general(hidden, expert_grad, (((0,), (0,)), ((), ())), preferred_element_type=jnp.float32).astype(jnp.bfloat16)
    hidden_grad = sliced_sum(expert_grad.reshape(count_rows, N_DP, width_slice), down_matrix.reshape(FF, N_DP, width_slice), "rsk,fsk->srf")
    gate_part = hidden_grad * up_pre * sigmoid_gate * (1.0 + gate_pre * (1.0 - sigmoid_gate))
    up_part = hidden_grad * activated
    act_grad = jnp.concatenate([gate_part, up_part], axis=1).astype(jnp.bfloat16)
    gate_up_gradient = lax.dot_general(restored, act_grad, (((0,), (0,)), ((), ())), preferred_element_type=jnp.float32).astype(jnp.bfloat16)
    input_grad = lax.dot_general(act_grad, gate_up, (((1,), (1,)), ((), ())), preferred_element_type=jnp.float32).astype(jnp.bfloat16)
    return expert_out, input_grad, gate_up_gradient, down_gradient


def reference(tokens, cotangent, expert_ids, gate_values, gate_up_weight, down_weight):
    sign_table = hadamard_signs(HB)
    coded_rows, block_scale = quantize(rotate_blocks(tokens, sign_table))
    restored_tokens = restore(coded_rows, block_scale)
    grouped = expert_ids.reshape(N_EXPERT, TOK_DEV, 2)
    slot_rank = jax.vmap(lambda block_ids: slot_positions(block_ids, EXPERTS))(grouped).reshape(TOKENS, 2)
    source = (jnp.arange(TOKENS, dtype=jnp.int32) // TOK_DEV)[:, None]
    target_row = ((expert_ids * N_EXPERT + source) * CAP + slot_rank).astype(jnp.int32)
    total_slots = EXPERTS * N_EXPERT * CAP
    flat_target = target_row.reshape(-1)
    restored_all = jnp.zeros((total_slots, D), jnp.bfloat16).at[flat_target].set(jnp.repeat(restored_tokens, 2, axis=0))
    weighted = (gate_values.reshape(-1)[:, None] * jnp.repeat(cotangent, 2, axis=0).astype(jnp.float32)).astype(jnp.bfloat16)
    grad_all = jnp.zeros((total_slots, D), jnp.bfloat16).at[flat_target].set(weighted)
    rows_each = N_EXPERT * CAP
    results = lax.map(expert_pass, (restored_all.reshape(EXPERTS, rows_each, D), grad_all.reshape(EXPERTS, rows_each, D), gate_up_weight, down_weight))
    expert_out, input_grad, gate_up_gradient, down_gradient = results
    picked_out = expert_out.reshape(total_slots, D)[target_row]
    layer_output = jnp.sum(gate_values[:, :, None] * picked_out.astype(jnp.float32), axis=1).astype(jnp.bfloat16)
    gate_gradient = jnp.sum(cotangent.astype(jnp.float32)[:, None, :] * picked_out.astype(jnp.float32), axis=2)
    picked_grad = input_grad.reshape(total_slots, D)[target_row]
    token_gradient = unrotate_pairs(picked_grad, sign_table).astype(jnp.bfloat16)
    return layer_output, token_gradient, gate_gradient, gate_up_gradient, down_gradient
```

```python
import functools

import jax
import jax.numpy as jnp
import numpy as np
from jax import lax
from jax.experimental import pallas as pl
from jax.experimental.pallas import tpu as pltpu
from jax.sharding import PartitionSpec as P

HB = 128
MESH = pl.DeviceIdType.MESH
BF = jnp.bfloat16
F32 = jnp.float32

NX, NY = 4, 4
NE = 32
CAP = 24
ROWS = NE * CAP
TOK = 192
KD = 256
FF = 1024
UC = 512
NU = 6
SH = 48


def sign_blocks():
    idx = np.arange(KD)
    common = (idx[:, None] & idx[None, :]) & (HB - 1)
    parity = np.zeros((KD, KD), np.int64)
    for bit in range(7):
        parity += (common >> bit) & 1
    signs = 1 - 2 * (parity & 1)
    return np.where((idx[:, None] // HB) == (idx[None, :] // HB), signs, 0)


def dot_nn(a, b):
    return lax.dot_general(a, b, (((1,), (0,)), ((), ())), preferred_element_type=F32)


def dot_nt(a, b):
    return lax.dot_general(a, b, (((1,), (1,)), ((), ())), preferred_element_type=F32)


def dot_tn(a, b):
    return lax.dot_general(a, b, (((0,), (0,)), ((), ())), preferred_element_type=F32)


def kernel(
    tok_ref, cot_ref, ids_ref, gate_ref, w_ref, dn_ref, sign_ref,
    lo_ref, tg_ref, gg_ref, gu_ref, dg_ref,
    send_x, send_g, send_o, send_i, got_x, got_g, got_o, got_i,
    xs, gs, xt, gt, hits,
    part, r1, r2, q, yr, gu_keep, full, acc_o, acc_i, gx, gy,
    s_a2a, r_a2a, s_x1, s_x2, s_y, s_ya, s_xa1, s_xa2,
    m_x1, m_x2, m_y, m_ya, m_xa1, m_xa2, s_gate, m_gate,
):
    dp = lax.axis_index("dp")
    me = lax.axis_index("expert")
    x = lax.rem(dp, NX)
    y = lax.div(dp, NX)
    xr, xo, xl = lax.rem(x + 1, NX), lax.rem(x + 2, NX), lax.rem(x + 3, NX)

    def at_x(other):
        return (y * NX + other, me)

    def at_y(other):
        return (other * NX + x, me)

    def send(src, dst, send_sem, recv_sem, device):
        pltpu.make_async_remote_copy(
            src_ref=src, dst_ref=dst, send_sem=send_sem, recv_sem=recv_sem,
            device_id=device, device_id_type=MESH,
        ).start()

    def wait_for(sem, ref):
        pltpu.make_async_copy(ref, ref, sem).wait()

    barrier = pltpu.get_barrier_semaphore()

    def greet(i, _):
        pl.semaphore_signal(
            barrier, inc=1, device_id=(dp, lax.rem(me + i, NE)), device_id_type=MESH
        )
        return 0

    lax.fori_loop(1, NE, greet, 0)
    for other in (xr, xo, xl):
        pl.semaphore_signal(barrier, inc=1, device_id=at_x(other), device_id_type=MESH)
    for j in (1, 2, 3):
        pl.semaphore_signal(
            barrier, inc=1, device_id=at_y(lax.rem(y + j, NY)), device_id_type=MESH
        )

    turned = dot_nn(tok_ref[...], sign_ref[...]) * (HB ** -0.5)
    pieces = []
    for b in range(KD // HB):
        block = turned[:, b * HB:(b + 1) * HB]
        top = jnp.max(jnp.abs(block), axis=1, keepdims=True) + 1e-06
        scale = jnp.broadcast_to(top, block.shape).astype(BF).astype(F32)
        coded = (block / scale).astype(BF)
        pieces.append((coded.astype(F32) * scale).astype(BF))
    restored = jnp.concatenate(pieces, axis=1)

    lanes = lax.broadcasted_iota(jnp.int32, (TOK, 128), 1)
    one0 = jnp.where(ids_ref[:, 0:1] == lanes, 1.0, 0.0)
    one1 = jnp.where(ids_ref[:, 1:2] == lanes, 1.0, 0.0)
    below = jnp.where(
        lax.broadcasted_iota(jnp.int32, (TOK, TOK), 0)
        > lax.broadcasted_iota(jnp.int32, (TOK, TOK), 1),
        1.0, 0.0,
    ).astype(BF)
    earlier = dot_nn(below, (one0 + one1).astype(BF))
    row_lanes = lax.broadcasted_iota(jnp.int32, (TOK, ROWS), 1)
    for k, one in enumerate((one0, one1)):
        rank = jnp.sum(one * earlier, axis=1, keepdims=True).astype(jnp.int32)
        target = ids_ref[:, k:k + 1] * CAP + rank
        hits[k] = jnp.where(target == row_lanes, 1.0, 0.0).astype(BF)

    both = (hits[0].astype(F32) + hits[1].astype(F32)).astype(BF)
    send_x[...] = dot_tn(both, restored).reshape(NE, CAP, KD).astype(BF)

    pl.semaphore_wait(barrier, NE - 1 + 6)

    def scatter(src, dst, n):
        def one_peer(i, _):
            peer = lax.rem(me + i, NE)
            send(src.at[peer], dst.at[me], s_a2a.at[n], r_a2a.at[n], (dp, peer))
            return 0

        lax.fori_loop(1, NE, one_peer, 0)
        dst[me] = src[me]

    def arrived(dst, n):
        wait_for(r_a2a.at[n], dst.at[pl.ds(0, NE - 1)])
        return dst[...].astype(F32).reshape(ROWS, KD).astype(BF)

    scatter(send_x, got_x, 0)

    cot = cot_ref[...].astype(F32)
    w0 = (gate_ref[:, 0:1] * cot).astype(BF)
    w1 = (gate_ref[:, 1:2] * cot).astype(BF)
    sent = dot_tn(hits[0], w0) + dot_tn(hits[1], w1)
    send_g[...] = sent.reshape(NE, CAP, KD).astype(BF)
    scatter(send_g, got_g, 1)

    def x1_send(u):
        send(part.at[u, pl.ds(4 * xo, 2)], r1.at[u, 0], s_x1, m_x1.at[u], at_x(xr))
        send(part.at[u, pl.ds(4 * xo + 2, 2)], r1.at[u, 1], s_x1, m_x1.at[u], at_x(xl))
        send(part.at[u, pl.ds(4 * xr + 2, 2)], r2.at[u, 0, pl.ds(2, 2)], s_x2, m_x2.at[u], at_x(xr))
        send(part.at[u, pl.ds(4 * xl, 2)], r2.at[u, 1, pl.ds(0, 2)], s_x2, m_x2.at[u], at_x(xl))

    def x1_pass(u):
        wait_for(m_x1.at[u], r1.at[u])
        lower = pl.ds(4 * xr, 2)
        part[u, lower] = (part[u, lower].astype(F32) + r1[u, 0].astype(F32)).astype(BF)
        send(part.at[u, lower], r2.at[u, 0, pl.ds(0, 2)], s_x2, m_x2.at[u], at_x(xr))
        upper = pl.ds(4 * xl + 2, 2)
        part[u, upper] = (part[u, upper].astype(F32) + r1[u, 1].astype(F32)).astype(BF)
        send(part.at[u, upper], r2.at[u, 1, pl.ds(2, 2)], s_x2, m_x2.at[u], at_x(xl))

    def x2_sum(u):
        wait_for(m_x2.at[u], r2.at[u])
        own = part[u, pl.ds(4 * x, 4)].astype(F32)
        q[u] = (own + r2[u, 0].astype(F32) + r2[u, 1].astype(F32)).astype(BF)
        for j in (1, 2, 3):
            other = lax.rem(y + j, NY)
            send(q.at[u, other], yr.at[u, j - 1], s_y, m_y.at[u], at_y(other))

    def y_sum(u):
        wait_for(m_y.at[u], yr.at[u])
        total = q[u, y].astype(F32) + yr[u, 0].astype(F32)
        return total + yr[u, 1].astype(F32) + yr[u, 2].astype(F32)

    home = 4 * x + y

    def ya_send(a):
        for j in (1, 2, 3):
            send(full.at[a, home], full.at[a, home], s_ya, m_ya.at[a], at_y(lax.rem(y + j, NY)))

    def xa1_send(a):
        wait_for(m_ya.at[a], yr.at[a])
        mine = pl.ds(4 * x, 4)
        for other in (xr, xl):
            send(full.at[a, mine], full.at[a, mine], s_xa1, m_xa1.at[a], at_x(other))

    def xa1_pass(a):
        wait_for(m_xa1.at[a], r2.at[a])
        lower, upper = pl.ds(4 * xl, 2), pl.ds(4 * xr + 2, 2)
        send(full.at[a, lower], full.at[a, lower], s_xa2, m_xa2.at[a], at_x(xr))
        send(full.at[a, upper], full.at[a, upper], s_xa2, m_xa2.at[a], at_x(xl))

    def gathered(a):
        wait_for(m_xa2.at[a], r1.at[a])

    def forward_part(c):
        for half in range(2):
            cols = slice(half * FF + 256 * c, half * FF + 256 * c + 256)
            out = dot_nn(xs[...], w_ref[:, cols]).astype(BF)
            part[c, :, :, 256 * half:256 * half + 256] = out.reshape(16, SH, 256)

    def backward_part(d):
        out = dot_nt(gs[...], dn_ref[UC * d:UC * d + UC, :]).astype(BF)
        part[4 + d] = out.reshape(16, SH, UC)

    def make_hidden(c):
        total = y_sum(c)
        gu_keep[c] = total
        gate, up = total[:, :256], total[:, 256:]
        hidden = (gate * jax.nn.sigmoid(gate)) * up
        a, half = c // 2, c % 2
        full[a, home, :, 256 * half:256 * half + 256] = hidden.astype(BF)

    def make_act(d):
        total = y_sum(4 + d)
        for half in range(2):
            c = 2 * d + half
            grad = total[:, 256 * half:256 * half + 256]
            gate, up = gu_keep[c, :, :256], gu_keep[c, :, 256:]
            sig = jax.nn.sigmoid(gate)
            cols = slice(256 * half, 256 * half + 256)
            full[2 + 2 * d, home, :, cols] = (grad * up * sig * (1.0 + gate * (1.0 - sig))).astype(BF)
            full[3 + 2 * d, home, :, cols] = (grad * (gate * sig)).astype(BF)

    def whole(a):
        return full[a].reshape(ROWS, UC)

    def use_hidden(a):
        gathered(a)
        rows = slice(UC * a, UC * a + UC)
        out = dot_nn(whole(a), dn_ref[rows, :])
        if a == 0:
            acc_o[...] = out
        else:
            send_o[...] = (acc_o[...] + out).reshape(NE, CAP, KD).astype(BF)
            scatter(send_o, got_o, 2)

    def hidden_weights(a):
        rows = slice(UC * a, UC * a + UC)
        dg_ref[rows, :] = dot_nn(gt[...], whole(a)).T.astype(BF)

    act_columns = {2: 0, 3: FF, 4: UC, 5: FF + UC}

    def use_act(a):
        gathered(a)
        cols = slice(act_columns[a], act_columns[a] + UC)
        out = dot_nt(whole(a), w_ref[:, cols])
        if a == 2:
            acc_i[...] = out
        elif a < 5:
            acc_i[...] += out
        else:
            send_i[...] = (acc_i[...] + out).reshape(NE, CAP, KD).astype(BF)
            scatter(send_i, got_i, 3)

    def act_weights(a):
        cols = slice(act_columns[a], act_columns[a] + UC)
        gu_ref[:, cols] = dot_nn(xt[...], whole(a)).astype(BF)

    xs[...] = arrived(got_x, 0)
    for c in range(4):
        forward_part(c)
        x1_send(c)
    x1_pass(0)
    x1_pass(1)
    gs[...] = arrived(got_g, 1)
    for d in range(2):
        backward_part(d)
        x1_send(4 + d)
    x1_pass(2)
    x2_sum(0)
    x1_pass(3)
    x2_sum(1)
    xt[...] = xs[...].T
    gt[...] = gs[...].T
    make_hidden(0)
    x1_pass(4)
    x2_sum(2)
    make_hidden(1)
    ya_send(0)
    x1_pass(5)
    x2_sum(3)
    make_hidden(2)
    xa1_send(0)
    x2_sum(4)
    make_hidden(3)
    ya_send(1)
    x2_sum(5)
    make_act(0)
    ya_send(2)
    ya_send(3)
    xa1_send(1)
    xa1_pass(0)
    make_act(1)
    ya_send(4)
    ya_send(5)
    xa1_send(2)
    xa1_send(3)
    xa1_pass(1)
    use_hidden(0)
    xa1_send(4)
    xa1_send(5)
    use_hidden(1)
    xa1_pass(2)
    hidden_weights(0)
    xa1_pass(3)
    hidden_weights(1)
    use_act(2)
    act_weights(2)
    xa1_pass(4)
    use_act(3)
    xa1_pass(5)
    act_weights(3)

    back = arrived(got_o, 2)
    p0, p1 = dot_nn(hits[0], back), dot_nn(hits[1], back)
    lo_ref[...] = (gate_ref[:, 0:1] * p0 + gate_ref[:, 1:2] * p1).astype(BF)
    ones = jnp.ones((8, KD), F32)

    def lane_sums(values):
        return lax.dot_general(
            ones, values, (((1,), (1,)), ((), ())),
            precision=lax.Precision.HIGHEST, preferred_element_type=F32,
        )

    cot_again = cot_ref[...].astype(F32)
    first = lax.broadcasted_iota(jnp.int32, (8, TOK), 0) == 0
    gx[x] = jnp.where(first, lane_sums(cot_again * p0), lane_sums(cot_again * p1))
    for j, other in enumerate((xr, xo, xl)):
        send(gx.at[x], gx.at[x], s_gate.at[0, j], m_gate.at[0, x], at_x(other))
    use_act(4)
    act_weights(4)
    for other in (xr, xo, xl):
        wait_for(m_gate.at[0, other], gx.at[other])
    gy[y] = (gx[0] + gx[1]) + (gx[2] + gx[3])
    for j in (1, 2, 3):
        send(gy.at[y], gy.at[y], s_gate.at[1, j - 1], m_gate.at[1, y], at_y(lax.rem(y + j, NY)))
    use_act(5)
    act_weights(5)
    for j in (1, 2, 3):
        other = lax.rem(y + j, NY)
        wait_for(m_gate.at[1, other], gy.at[other])
    gg_ref[...] = (gy[0] + gy[1]) + (gy[2] + gy[3])

    back = arrived(got_i, 3)
    pair = dot_nn(hits[0], back) + dot_nn(hits[1], back)
    high = pair.astype(BF)
    low = (pair - high.astype(F32)).astype(BF)
    signs = sign_ref[...]
    tg_ref[...] = ((dot_nn(high, signs) + dot_nn(low, signs)) * (HB ** -0.5)).astype(BF)

    for n, buf in enumerate((send_x, send_g, send_o, send_i)):
        wait_for(s_a2a.at[n], buf.at[pl.ds(0, NE - 1)])
    wait_for(s_x1, r1)
    wait_for(s_x2, r2)
    wait_for(s_y, yr)
    wait_for(s_ya, yr)
    wait_for(s_xa1, r2)
    wait_for(s_xa2, r1)
    for j in range(3):
        wait_for(s_gate.at[0, j], gx.at[0])
        wait_for(s_gate.at[1, j], gy.at[0])


def per_device(tokens, cotangent, expert_ids, gate_values, gate_up_weight, down_weight):
    vmem = pl.BlockSpec(memory_space=pltpu.VMEM)
    slabs = pltpu.VMEM((NE, CAP, KD), BF)
    dma = pltpu.SemaphoreType.DMA
    lo, tg, gg, gu, dg = pl.pallas_call(
        kernel,
        out_shape=(
            jax.ShapeDtypeStruct((TOK, KD), BF),
            jax.ShapeDtypeStruct((TOK, KD), BF),
            jax.ShapeDtypeStruct((8, TOK), F32),
            jax.ShapeDtypeStruct((KD, 2 * FF), BF),
            jax.ShapeDtypeStruct((FF, KD), BF),
        ),
        in_specs=[vmem] * 7,
        out_specs=[vmem] * 5,
        scratch_shapes=[
            slabs, slabs, slabs, slabs, slabs, slabs, slabs, slabs,
            pltpu.VMEM((ROWS, KD), BF), pltpu.VMEM((ROWS, KD), BF),
            pltpu.VMEM((KD, ROWS), BF), pltpu.VMEM((KD, ROWS), BF),
            pltpu.VMEM((2, TOK, ROWS), BF),
            pltpu.VMEM((NU, 16, SH, UC), BF),
            pltpu.VMEM((NU, 2, 2, SH, UC), BF),
            pltpu.VMEM((NU, 2, 4, SH, UC), BF),
            pltpu.VMEM((NU, 4, SH, UC), BF),
            pltpu.VMEM((NU, 3, SH, UC), BF),
            pltpu.VMEM((4, SH, UC), F32),
            pltpu.VMEM((NU, 16, SH, UC), BF),
            pltpu.VMEM((ROWS, KD), F32), pltpu.VMEM((ROWS, KD), F32),
            pltpu.VMEM((NX, 8, TOK), F32), pltpu.VMEM((NY, 8, TOK), F32),
            dma((4,)), dma((4,)),
            dma, dma, dma, dma, dma, dma,
            dma((NU,)), dma((NU,)), dma((NU,)), dma((NU,)), dma((NU,)), dma((NU,)),
            dma((2, 3)), dma((2, 4)),
        ],
        compiler_params=pltpu.CompilerParams(
            collective_id=0, has_side_effects=True, vmem_limit_bytes=56 * 1024 * 1024
        ),
        cost_estimate=pl.CostEstimate(
            flops=2 * ROWS * KD * 9 * FF, bytes_accessed=6 * 1024 * 1024, transcendentals=ROWS * FF
        ),
    )(
        tokens, cotangent, expert_ids, gate_values, gate_up_weight[0], down_weight[0],
        jnp.asarray(sign_blocks(), BF),
    )
    return lo, tg, gg[:2].T, gu[None], dg[None]


def solution(mesh):
    return jax.shard_map(
        per_device,
        mesh=mesh,
        in_specs=(
            P("expert", "dp"),
            P("expert", "dp"),
            P("expert", None),
            P("expert", None),
            P("expert", "dp", None),
            P("expert", None, "dp"),
        ),
        out_specs=(
            P("expert", "dp"),
            P("expert", "dp"),
            P("expert", None),
            P("expert", "dp", None),
            P("expert", None, "dp"),
        ),
        check_vma=False,
    )
```

```python
import functools

import jax
import jax.numpy as jnp
from jax import lax
from jax.experimental import pallas as pl
from jax.experimental.pallas import tpu as pltpu
from jax.sharding import PartitionSpec as P

HB = 128
MESH = pl.DeviceIdType.MESH
BF = jnp.bfloat16
F32 = jnp.float32

NX, NY = 4, 4
NE = 32
CAP = 24
ROWS = NE * CAP
TOK = 192
KD = 256
FF = 1024
UC = 512
NU = 6
NH, NA = 2, 3
SH = 48
AR = SH // NA


def dot_nn(a, b):
    return lax.dot_general(a, b, (((1,), (0,)), ((), ())), preferred_element_type=F32)


def dot_nt(a, b):
    return lax.dot_general(a, b, (((1,), (1,)), ((), ())), preferred_element_type=F32)


def dot_tn(a, b):
    return lax.dot_general(a, b, (((0,), (0,)), ((), ())), preferred_element_type=F32)


def signs_of_block():
    common = jnp.bitwise_and(
        lax.broadcasted_iota(jnp.int32, (HB, HB), 0), lax.broadcasted_iota(jnp.int32, (HB, HB), 1)
    )
    for shift in (4, 2, 1):
        common = jnp.bitwise_xor(common, jnp.right_shift(common, shift))
    return (1 - 2 * jnp.bitwise_and(common, 1)).astype(F32).astype(BF)


def kernel(
    tok_ref, cot_ref, ids_ref, gate_ref, w_hbm, dn_hbm,
    lo_ref, tg_ref, gg_ref, gu_hbm, dg_hbm,
    w_ref, dn_ref, gu_ref, dg_ref, gu_acc, signs,
    send_x, send_g, send_o, send_i, got_x, got_g, got_o, got_i,
    xs, gs, xt, gt, hits, hits_t,
    part, r1, r2, q, yr, gu_keep, full, fa, acc_o, ig, gx, gy,
    s_local, s_a2a, r_a2a, s_x1, s_x2, s_y, m_x1, m_x2, m_y,
    s_ya, s_xa1, s_xa2, m_ya, m_xa1, m_xa2, s_gate, m_gate,
):
    dp = lax.axis_index("dp")
    me = lax.axis_index("expert")
    x = lax.rem(dp, NX)
    y = lax.div(dp, NX)
    xr, xo, xl = lax.rem(x + 1, NX), lax.rem(x + 2, NX), lax.rem(x + 3, NX)

    def at_x(other):
        return (y * NX + other, me)

    def at_y(other):
        return (other * NX + x, me)

    def send(src, dst, send_sem, recv_sem, device):
        pltpu.make_async_remote_copy(
            src_ref=src, dst_ref=dst, send_sem=send_sem, recv_sem=recv_sem,
            device_id=device, device_id_type=MESH,
        ).start()

    def wait_for(sem, ref):
        pltpu.make_async_copy(ref, ref, sem).wait()

    barrier = pltpu.get_barrier_semaphore()

    def greet(i, _):
        pl.semaphore_signal(
            barrier, inc=1, device_id=(dp, lax.rem(me + i, NE)), device_id_type=MESH
        )
        return 0

    lax.fori_loop(1, NE, greet, 0)
    for other in (xr, xo, xl):
        pl.semaphore_signal(barrier, inc=1, device_id=at_x(other), device_id_type=MESH)
    for j in (1, 2, 3):
        pl.semaphore_signal(
            barrier, inc=1, device_id=at_y(lax.rem(y + j, NY)), device_id_type=MESH
        )
    fetch_w = pltpu.make_async_copy(w_hbm, w_ref, s_local.at[0])
    fetch_dn = pltpu.make_async_copy(dn_hbm, dn_ref, s_local.at[1])
    fetch_w.start()
    fetch_dn.start()

    places = lax.broadcasted_iota(jnp.int32, (NE, TOK), 0)
    one0 = jnp.where(ids_ref[0:1, :] == places, 1.0, 0.0)
    one1 = jnp.where(ids_ref[1:2, :] == places, 1.0, 0.0)
    before = jnp.where(
        lax.broadcasted_iota(jnp.int32, (TOK, TOK), 0)
        < lax.broadcasted_iota(jnp.int32, (TOK, TOK), 1),
        1.0, 0.0,
    ).astype(BF)
    earlier = dot_nn((one0 + one1).astype(BF), before)
    targets = []
    for k, one in enumerate((one0, one1)):
        rank = jnp.sum(one * earlier, axis=0, keepdims=True)
        targets.append(ids_ref[k:k + 1, :].astype(F32) * CAP + rank)
    rows = lax.broadcasted_iota(jnp.int32, (ROWS, TOK), 0)
    hit0 = targets[0].astype(jnp.int32) == rows
    hit1 = targets[1].astype(jnp.int32) == rows
    hits_t[0] = jnp.where(hit0, 1.0, 0.0).astype(BF)
    hits_t[1] = jnp.where(hit1, 1.0, 0.0).astype(BF)
    both = jnp.where(jnp.logical_or(hit0, hit1), 1.0, 0.0).astype(BF)

    signs[...] = signs_of_block()
    pieces = []
    for b in range(KD // HB):
        block = dot_nn(tok_ref[:, b * HB:(b + 1) * HB], signs[...]) * (HB ** -0.5)
        top = jnp.max(jnp.abs(block), axis=1, keepdims=True) + 1e-06
        scale = jnp.broadcast_to(top, block.shape).astype(BF).astype(F32)
        coded = (block / scale).astype(BF)
        pieces.append((coded.astype(F32) * scale).astype(BF))
    restored = jnp.concatenate(pieces, axis=1)
    send_x[...] = dot_nn(both, restored).reshape(NE, CAP, KD).astype(BF)

    pl.semaphore_wait(barrier, NE - 1 + 6)

    def scatter(src, dst, n):
        def one_peer(i, _):
            peer = lax.rem(me + i, NE)
            send(src.at[peer], dst.at[me], s_a2a.at[n], r_a2a.at[n], (dp, peer))
            return 0

        lax.fori_loop(1, NE, one_peer, 0)
        dst[me] = src[me]

    def arrived(dst, n):
        wait_for(r_a2a.at[n], got_x.at[pl.ds(0, NE - 1)])
        return dst[...].astype(F32).reshape(ROWS, KD).astype(BF)

    scatter(send_x, got_x, 0)

    small = jnp.concatenate(
        [targets[0], targets[1], gate_ref[...], jnp.zeros((4, TOK), F32)], axis=0
    )
    columns = jnp.concatenate([small, jnp.zeros((8, 256 - TOK), F32)], axis=1).T[:TOK]
    gate0, gate1 = columns[:, 2:3], columns[:, 3:4]
    cot = cot_ref[...].astype(F32)
    sent = dot_nn(hits_t[0], (gate0 * cot).astype(BF)) + dot_nn(hits_t[1], (gate1 * cot).astype(BF))
    send_g[...] = sent.reshape(NE, CAP, KD).astype(BF)
    scatter(send_g, got_g, 1)
    row_lanes = lax.broadcasted_iota(jnp.int32, (TOK, ROWS), 1)
    for k in range(2):
        hits[k] = jnp.where(columns[:, k:k + 1].astype(jnp.int32) == row_lanes, 1.0, 0.0).astype(BF)

    def x1(u):
        send(part.at[u, pl.ds(4 * xo, 2)], r1.at[u, 0], s_x1, m_x1.at[u], at_x(xr))
        send(part.at[u, pl.ds(4 * xo + 2, 2)], r1.at[u, 1], s_x1, m_x1.at[u], at_x(xl))

    def x2_plain(u):
        send(part.at[u, pl.ds(4 * xr + 2, 2)], r2.at[u, 0, pl.ds(2, 2)], s_x2, m_x2.at[u], at_x(xr))
        send(part.at[u, pl.ds(4 * xl, 2)], r2.at[u, 1, pl.ds(0, 2)], s_x2, m_x2.at[u], at_x(xl))

    def x2_added(u):
        wait_for(m_x1.at[u], r1.at[u])
        lower = pl.ds(4 * xr, 2)
        part[u, lower] = (part[u, lower].astype(F32) + r1[u, 0].astype(F32)).astype(BF)
        send(part.at[u, lower], r2.at[u, 0, pl.ds(0, 2)], s_x2, m_x2.at[u], at_x(xr))
        upper = pl.ds(4 * xl + 2, 2)
        part[u, upper] = (part[u, upper].astype(F32) + r1[u, 1].astype(F32)).astype(BF)
        send(part.at[u, upper], r2.at[u, 1, pl.ds(2, 2)], s_x2, m_x2.at[u], at_x(xl))

    def x2_sum(u):
        wait_for(m_x2.at[u], r2.at[u])
        own = part[u, pl.ds(4 * x, 4)].astype(F32)
        q[u] = (own + r2[u, 0].astype(F32) + r2[u, 1].astype(F32)).astype(BF)
        for j in (2, 1, 3):
            other = lax.rem(y + j, NY)
            send(q.at[u, other], yr.at[u, j - 1], s_y, m_y.at[u], at_y(other))

    def y_sum(u):
        wait_for(m_y.at[u], yr.at[u])
        total = q[u, y].astype(F32) + yr[u, 0].astype(F32)
        return total + yr[u, 1].astype(F32) + yr[u, 2].astype(F32)

    home = 4 * x + y

    def unit(a):
        return full.at[a] if a < NH else fa.at[a - NH]

    def ya(a):
        block = unit(a).at[home]
        for j in (2, 1, 3):
            send(block, block, s_ya.at[a], m_ya.at[a], at_y(lax.rem(y + j, NY)))

    def xa1(a):
        wait_for(m_ya.at[a], unit(a).at[pl.ds(0, 3)])
        mine = unit(a).at[pl.ds(4 * x, 4)]
        for other in (xr, xl):
            send(mine, mine, s_xa1.at[a], m_xa1.at[a], at_x(other))

    def xa2(a):
        wait_for(m_xa1.at[a], unit(a).at[pl.ds(0, 8)])
        lower, upper = unit(a).at[pl.ds(4 * xl, 2)], unit(a).at[pl.ds(4 * xr + 2, 2)]
        send(lower, lower, s_xa2.at[a], m_xa2.at[a], at_x(xr))
        send(upper, upper, s_xa2.at[a], m_xa2.at[a], at_x(xl))

    def gathered(a):
        wait_for(m_xa2.at[a], unit(a).at[pl.ds(0, 4)])

    def forward_part(c):
        left = xs[...].reshape(ROWS, KD)
        for half in range(2):
            cols = slice(half * FF + 256 * c, half * FF + 256 * c + 256)
            out = dot_nn(left, w_ref[:, cols]).astype(BF)
            part[c, :, :, 256 * half:256 * half + 256] = out.reshape(16, SH, 256)

    def backward_part(d):
        out = dot_nt(gs[...], dn_ref[UC * d:UC * d + UC, :]).astype(BF)
        part[4 + d] = out.reshape(16, SH, UC)

    def make_hidden(c):
        total = y_sum(c)
        gu_keep[c] = total
        gate, up = total[:, :256], total[:, 256:]
        hidden = (gate * jax.nn.sigmoid(gate)) * up
        a, half = c // 2, c % 2
        full[a, home, :, 256 * half:256 * half + 256] = hidden.astype(BF)

    def make_act(d):
        total = y_sum(4 + d)
        for half in range(2):
            c = 2 * d + half
            grad = total[:, 256 * half:256 * half + 256]
            gate, up = gu_keep[c, :, :256], gu_keep[c, :, 256:]
            sig = jax.nn.sigmoid(gate)
            of_gate = (grad * up * sig * (1.0 + gate * (1.0 - sig))).astype(BF)
            of_up = (grad * (gate * sig)).astype(BF)
            for r in range(NA):
                some = slice(AR * r, AR * r + AR)
                fa[r, home, :, 256 * c:256 * c + 256] = of_gate[some]
                fa[r, home, :, FF + 256 * c:FF + 256 * c + 256] = of_up[some]

    def use_hidden(a):
        gathered(a)
        out = dot_nn(full[a].reshape(ROWS, UC), dn_ref[UC * a:UC * a + UC, :])
        if a == 0:
            acc_o[...] = out
        else:
            send_o[...] = (acc_o[...] + out).reshape(NE, CAP, KD).astype(BF)
            scatter(send_o, got_o, 2)

    def hidden_weights(a):
        grads = dot_nn(gt[...], full[a].reshape(ROWS, UC))
        dg_ref[UC * a:UC * a + UC, :] = grads.T.astype(BF)

    def use_act(r):
        gathered(NH + r)
        out = dot_nt(fa[r].reshape(16 * AR, 2 * FF), w_ref[...])
        ig[:, AR * r:AR * r + AR, :] = out.reshape(16, AR, KD)

    def act_weights(r):
        for n in range(4):
            cols = slice(UC * n, UC * n + UC)
            grads = dot_nn(xt[r], fa[r, :, :, cols].reshape(16 * AR, UC))
            if r == 0:
                gu_acc[:, cols] = grads
            elif r < NA - 1:
                gu_acc[:, cols] += grads
            else:
                gu_ref[:, cols] = (gu_acc[:, cols] + grads).astype(BF)

    def scatter_half(core):
        send_i[:, core] = ig[:, CAP * core:CAP * core + CAP, :].astype(BF)
        pair, mine = lax.div(me, 2), lax.rem(me, 2)

        def one_peer(i, _):
            to = lax.rem(pair + i, NE // 2)

            @pl.when(jnp.logical_or(to != pair, mine != core))
            def _():
                send(
                    send_i.at[to, core], got_i.at[pair, mine],
                    s_a2a.at[3], r_a2a.at[3], (dp, 2 * to + core),
                )

            return 0

        lax.fori_loop(0, NE // 2, one_peer, 0)

        @pl.when(mine == core)
        def _():
            got_i[pair, core] = send_i[pair, core]

    fetch_w.wait()
    fetch_dn.wait()
    xs[...] = arrived(got_x, 0).reshape(16, SH, KD)
    forward_part(0)
    x1(0)
    x2_plain(0)
    forward_part(1)
    x1(1)
    forward_part(2)
    x2_added(0)
    x2_plain(1)
    x1(2)
    forward_part(3)
    x2_added(1)
    x2_plain(2)
    x1(3)
    x2_sum(0)
    gs[...] = arrived(got_g, 1)
    backward_part(0)
    x2_added(2)
    x2_plain(3)
    x1(4)
    x2_sum(1)
    backward_part(1)
    make_hidden(0)
    x2_added(3)
    x2_plain(4)
    x1(5)
    x2_sum(2)
    make_hidden(1)
    ya(0)
    x2_added(4)
    x2_plain(5)
    x2_sum(3)
    make_hidden(2)
    x2_added(5)
    xa1(0)
    x2_sum(4)
    make_hidden(3)
    ya(1)
    x2_sum(5)
    make_act(0)
    xa1(1)
    xa2(0)
    make_act(1)
    ya(2)
    ya(3)
    ya(4)
    for r in range(NA):
        xt[r] = xs[:, AR * r:AR * r + AR, :].reshape(16 * AR, KD).T
    gt[...] = gs[...].T
    xa2(1)
    xa1(2)
    use_hidden(0)
    xa1(3)
    use_hidden(1)
    xa1(4)
    xa2(2)
    hidden_weights(0)
    hidden_weights(1)
    put_dg = pltpu.make_async_copy(dg_ref, dg_hbm, s_local.at[2])
    put_dg.start()
    xa2(3)
    use_act(0)
    act_weights(0)
    xa2(4)

    back = arrived(got_o, 2)
    p0, p1 = dot_nn(hits[0], back), dot_nn(hits[1], back)
    lo_ref[...] = (gate0 * p0 + gate1 * p1).astype(BF)
    ones = jnp.ones((8, KD), F32)

    def lane_sums(values):
        return lax.dot_general(
            ones, values, (((1,), (1,)), ((), ())),
            precision=lax.Precision.HIGHEST, preferred_element_type=F32,
        )

    cot_again = cot_ref[...].astype(F32)
    first = lax.broadcasted_iota(jnp.int32, (8, TOK), 0) == 0
    gx[x] = jnp.where(first, lane_sums(cot_again * p0), lane_sums(cot_again * p1))
    for j, other in enumerate((xr, xo, xl)):
        send(gx.at[x], gx.at[x], s_gate.at[0, j], m_gate.at[0, x], at_x(other))
    use_act(1)
    scatter_half(0)
    act_weights(1)
    for other in (xr, xo, xl):
        wait_for(m_gate.at[0, other], gx.at[other])
    gy[y] = (gx[0] + gx[1]) + (gx[2] + gx[3])
    for j in (1, 2, 3):
        send(gy.at[y], gy.at[y], s_gate.at[1, j - 1], m_gate.at[1, y], at_y(lax.rem(y + j, NY)))
    use_act(2)
    scatter_half(1)
    act_weights(2)
    put_gu = pltpu.make_async_copy(gu_ref, gu_hbm, s_local.at[3])
    put_gu.start()
    for j in (1, 2, 3):
        other = lax.rem(y + j, NY)
        wait_for(m_gate.at[1, other], gy.at[other])
    gg_ref[...] = ((gy[0] + gy[1]) + (gy[2] + gy[3]))[0:2]

    for n, buf in enumerate((send_x, send_g, send_o)):
        wait_for(s_a2a.at[n], buf.at[pl.ds(0, NE - 1)])
    wait_for(s_x1, r1)
    wait_for(s_x2, r2)
    wait_for(s_y, yr)
    for a in range(NH + NA):
        wait_for(s_ya.at[a], unit(a).at[pl.ds(0, 3)])
        wait_for(s_xa1.at[a], unit(a).at[pl.ds(0, 8)])
        wait_for(s_xa2.at[a], unit(a).at[pl.ds(0, 4)])
    for j in range(3):
        wait_for(s_gate.at[0, j], gx.at[0])
        wait_for(s_gate.at[1, j], gy.at[0])
    put_dg.wait()

    back = arrived(got_i, 3)
    pair = dot_nn(hits[0], back) + dot_nn(hits[1], back)
    high = pair.astype(BF)
    low = (pair - high.astype(F32)).astype(BF)
    for b in range(KD // HB):
        cols = slice(b * HB, (b + 1) * HB)
        out = dot_nn(high[:, cols], signs[...]) + dot_nn(low[:, cols], signs[...])
        tg_ref[:, cols] = (out * (HB ** -0.5)).astype(BF)
    wait_for(s_a2a.at[3], send_x.at[pl.ds(0, NE - 1)])
    put_gu.wait()


def place_results(*refs):
    count = 5
    sources, targets, held = refs[:count], refs[count:2 * count], refs[2 * count:3 * count]
    s_in, s_out = refs[3 * count:]
    order = (3, 4, 0, 1, 2)
    fetch = {n: pltpu.make_async_copy(sources[n], held[n], s_in.at[n]) for n in order}
    put = {n: pltpu.make_async_copy(held[n], targets[n], s_out.at[n]) for n in order}
    for n in order:
        fetch[n].start()
    for n in order:
        fetch[n].wait()
        put[n].start()
    for n in order:
        put[n].wait()


def per_device(tokens, cotangent, expert_ids, gate_values, gate_up_weight, down_weight):
    vmem = pl.BlockSpec(memory_space=pltpu.VMEM)
    hbm = pl.BlockSpec(memory_space=pl.ANY)
    slabs = pltpu.VMEM((NE, CAP, KD), BF)
    dma = pltpu.SemaphoreType.DMA
    results = (
        jax.ShapeDtypeStruct((TOK, KD), BF),
        jax.ShapeDtypeStruct((TOK, KD), BF),
        jax.ShapeDtypeStruct((2, TOK), F32),
        jax.ShapeDtypeStruct((KD, 2 * FF), BF),
        jax.ShapeDtypeStruct((FF, KD), BF),
    )
    made = pl.pallas_call(
        kernel,
        out_shape=results,
        in_specs=[vmem] * 4 + [hbm] * 2,
        out_specs=[vmem] * 3 + [hbm] * 2,
        scratch_shapes=[
            pltpu.VMEM((KD, 2 * FF), BF), pltpu.VMEM((FF, KD), BF),
            pltpu.VMEM((KD, 2 * FF), BF), pltpu.VMEM((FF, KD), BF),
            pltpu.VMEM((KD, 2 * FF), F32), pltpu.VMEM((HB, HB), BF),
            slabs, slabs, slabs, pltpu.VMEM((NE // 2, 2, CAP, KD), BF),
            slabs, slabs, slabs, pltpu.VMEM((NE // 2, 2, CAP, KD), BF),
            pltpu.VMEM((16, SH, KD), BF), pltpu.VMEM((ROWS, KD), BF),
            pltpu.VMEM((NA, KD, 16 * AR), BF), pltpu.VMEM((KD, ROWS), BF),
            pltpu.VMEM((2, TOK, ROWS), BF), pltpu.VMEM((2, ROWS, TOK), BF),
            pltpu.VMEM((NU, 16, SH, UC), BF),
            pltpu.VMEM((NU, 2, 2, SH, UC), BF),
            pltpu.VMEM((NU, 2, 4, SH, UC), BF),
            pltpu.VMEM((NU, 4, SH, UC), BF),
            pltpu.VMEM((NU, 3, SH, UC), BF),
            pltpu.VMEM((4, SH, UC), F32),
            pltpu.VMEM((NH, 16, SH, UC), BF),
            pltpu.VMEM((NA, 16, AR, 2 * FF), BF),
            pltpu.VMEM((ROWS, KD), F32), pltpu.VMEM((16, SH, KD), F32),
            pltpu.VMEM((NX, 8, TOK), F32), pltpu.VMEM((NY, 8, TOK), F32),
            dma((4,)), dma((4,)), dma((4,)),
            dma, dma, dma, dma((NU,)), dma((NU,)), dma((NU,)),
            dma((NH + NA,)), dma((NH + NA,)), dma((NH + NA,)),
            dma((NH + NA,)), dma((NH + NA,)), dma((NH + NA,)),
            dma((2, 3)), dma((2, 4)),
        ],
        compiler_params=pltpu.CompilerParams(
            collective_id=0, has_side_effects=True, vmem_limit_bytes=56 * 1024 * 1024
        ),
        cost_estimate=pl.CostEstimate(
            flops=2 * ROWS * KD * 9 * FF, bytes_accessed=6 * 1024 * 1024, transcendentals=ROWS * FF
        ),
    )(
        tokens, cotangent, expert_ids.T, gate_values.T, gate_up_weight[0], down_weight[0],
    )
    lo, tg, gg, gu, dg = pl.pallas_call(
        place_results,
        out_shape=results,
        in_specs=[hbm] * 5,
        out_specs=[hbm] * 5,
        scratch_shapes=[pltpu.VMEM(r.shape, r.dtype) for r in results] + [dma((5,)), dma((5,))],
    )(*made)
    return lo, tg, gg.T, gu[None], dg[None]


def solution(mesh):
    return jax.shard_map(
        per_device,
        mesh=mesh,
        in_specs=(
            P("expert", "dp"),
            P("expert", "dp"),
            P("expert", None),
            P("expert", None),
            P("expert", "dp", None),
            P("expert", None, "dp"),
        ),
        out_specs=(
            P("expert", "dp"),
            P("expert", "dp"),
            P("expert", None),
            P("expert", "dp", None),
            P("expert", None, "dp"),
        ),
        check_vma=False,
    )
```

```python
import functools

import jax
import jax.numpy as jnp
from jax import lax
from jax.experimental import pallas as pl
from jax.experimental.pallas import tpu as pltpu
from jax.sharding import PartitionSpec as P

HB = 128
MESH = pl.DeviceIdType.MESH
BF = jnp.bfloat16
F32 = jnp.float32

NX, NY = 4, 4
NE = 32
CAP = 24
ROWS = NE * CAP
TOK = 192
KD = 256
FF = 1024
FX = FF // NX
NU = 4
UR = ROWS // NU
SH = UR // NY
ND = 2


def dot_nn(a, b):
    return lax.dot_general(a, b, (((1,), (0,)), ((), ())), preferred_element_type=F32)


def dot_nt(a, b):
    return lax.dot_general(a, b, (((1,), (1,)), ((), ())), preferred_element_type=F32)


def dot_tn(a, b):
    return lax.dot_general(a, b, (((0,), (0,)), ((), ())), preferred_element_type=F32)


def signs_of_block():
    common = jnp.bitwise_and(
        lax.broadcasted_iota(jnp.int32, (HB, HB), 0), lax.broadcasted_iota(jnp.int32, (HB, HB), 1)
    )
    for shift in (4, 2, 1):
        common = jnp.bitwise_xor(common, jnp.right_shift(common, shift))
    return (1 - 2 * jnp.bitwise_and(common, 1)).astype(F32).astype(BF)


def kernel(
    tok_ref, cot_ref, ids_ref, gate_ref, w_hbm, dn_hbm,
    lo_ref, tg_ref, gg_ref, gu_hbm, dg_hbm,
    w_ref, dn_ref, gu_ref, dg_ref, gu_acc, signs, wx,
    send_x, send_g, send_o, send_i, got_x, got_g, got_o, got_i,
    xg, gs, xt, gt, hits, hits_t,
    pf, fb, fc, pv, r1, r2, qv, vb, vc, gu_keep, hid, act, gx, gy,
    s_local, s_a2a, r_a2a, s_w, m_w, s_xg1, s_xg2, m_xg1, m_xg2,
    s_f1, s_f2, m_f1, m_f2, s_x1, s_x2, m_x1, m_x2, s_v1, s_v2, m_v1, m_v2,
    s_ya1, s_ya2, s_xa1, s_xa2, m_ya1, m_ya2, m_xa1, m_xa2, s_gate, m_gate,
):
    dp = lax.axis_index("dp")
    me = lax.axis_index("expert")
    x = lax.rem(dp, NX)
    y = lax.div(dp, NX)
    xr, xo, xl = lax.rem(x + 1, NX), lax.rem(x + 2, NX), lax.rem(x + 3, NX)
    y1, y2, y3 = y + 1 - 2 * lax.rem(y, 2), lax.rem(y + 2, NY), NY - 1 - y

    def at_x(other):
        return (y * NX + other, me)

    def at_y(other):
        return (other * NX + x, me)

    def send(src, dst, send_sem, recv_sem, device):
        pltpu.make_async_remote_copy(
            src_ref=src, dst_ref=dst, send_sem=send_sem, recv_sem=recv_sem,
            device_id=device, device_id_type=MESH,
        ).start()

    def wait_for(sem, ref):
        pltpu.make_async_copy(ref, ref, sem).wait()

    barrier = pltpu.get_barrier_semaphore()

    def greet(i, _):
        pl.semaphore_signal(
            barrier, inc=1, device_id=(dp, lax.rem(me + i, NE)), device_id_type=MESH
        )
        return 0

    lax.fori_loop(1, NE, greet, 0)
    for other in (xr, xo, xl):
        pl.semaphore_signal(barrier, inc=1, device_id=at_x(other), device_id_type=MESH)
    for j in (1, 2, 3):
        pl.semaphore_signal(
            barrier, inc=1, device_id=at_y(lax.rem(y + j, NY)), device_id_type=MESH
        )
    fetch_w = pltpu.make_async_copy(w_hbm, w_ref, s_local.at[0])
    fetch_dn = pltpu.make_async_copy(dn_hbm, dn_ref, s_local.at[1])
    fetch_w.start()
    fetch_dn.start()

    def own_columns(half, other):
        return w_hbm.at[:, pl.ds(pl.multiple_of(half * FF + FX * other, FX), FX)]

    keep = [
        pltpu.make_async_copy(own_columns(half, x), wx.at[x, half], s_local.at[4 + half])
        for half in range(2)
    ]
    for copy in keep:
        copy.start()

    places = lax.broadcasted_iota(jnp.int32, (NE, TOK), 0)
    one0 = jnp.where(ids_ref[0:1, :] == places, 1.0, 0.0)
    one1 = jnp.where(ids_ref[1:2, :] == places, 1.0, 0.0)
    before = jnp.where(
        lax.broadcasted_iota(jnp.int32, (TOK, TOK), 0)
        < lax.broadcasted_iota(jnp.int32, (TOK, TOK), 1),
        1.0, 0.0,
    ).astype(BF)
    earlier = dot_nn((one0 + one1).astype(BF), before)
    targets = []
    for k, one in enumerate((one0, one1)):
        rank = jnp.sum(one * earlier, axis=0, keepdims=True)
        targets.append(ids_ref[k:k + 1, :].astype(F32) * CAP + rank)
    rows = lax.broadcasted_iota(jnp.int32, (ROWS, TOK), 0)
    hit0 = targets[0].astype(jnp.int32) == rows
    hit1 = targets[1].astype(jnp.int32) == rows
    hits_t[0] = jnp.where(hit0, 1.0, 0.0).astype(BF)
    hits_t[1] = jnp.where(hit1, 1.0, 0.0).astype(BF)
    both = jnp.where(jnp.logical_or(hit0, hit1), 1.0, 0.0).astype(BF)

    pl.semaphore_wait(barrier, NE - 1 + 6)
    for half in range(2):
        for other in (xo, xr, xl):
            send(own_columns(half, other), wx.at[x, half], s_w, m_w, at_x(other))

    signs[...] = signs_of_block()
    pieces = []
    for b in range(KD // HB):
        block = dot_nn(tok_ref[:, b * HB:(b + 1) * HB], signs[...]) * (HB ** -0.5)
        top = jnp.max(jnp.abs(block), axis=1, keepdims=True) + 1e-06
        scale = jnp.broadcast_to(top, block.shape).astype(BF).astype(F32)
        coded = (block / scale).astype(BF)
        pieces.append((coded.astype(F32) * scale).astype(BF))
    restored = jnp.concatenate(pieces, axis=1)
    send_x[...] = dot_nn(both, restored).reshape(NE, CAP, KD).astype(BF)

    def scatter(src, dst, n):
        def one_peer(i, _):
            peer = lax.rem(me + i, NE)
            send(src.at[peer], dst.at[me], s_a2a.at[n], r_a2a.at[n], (dp, peer))
            return 0

        lax.fori_loop(1, NE, one_peer, 0)
        dst[me] = src[me]

    def arrived(dst, n):
        wait_for(r_a2a.at[n], got_x.at[pl.ds(0, NE - 1)])
        return dst[...].astype(F32).reshape(ROWS, KD).astype(BF)

    scatter(send_x, got_x, 0)

    small = jnp.concatenate(
        [targets[0], targets[1], gate_ref[...], jnp.zeros((4, TOK), F32)], axis=0
    )
    columns = jnp.concatenate([small, jnp.zeros((8, 256 - TOK), F32)], axis=1).T[:TOK]
    gate0, gate1 = columns[:, 2:3], columns[:, 3:4]
    cot = cot_ref[...].astype(F32)
    sent = dot_nn(hits_t[0], (gate0 * cot).astype(BF)) + dot_nn(hits_t[1], (gate1 * cot).astype(BF))
    send_g[...] = sent.reshape(NE, CAP, KD).astype(BF)
    scatter(send_g, got_g, 1)
    row_lanes = lax.broadcasted_iota(jnp.int32, (TOK, ROWS), 1)
    for k in range(2):
        hits[k] = jnp.where(columns[:, k:k + 1].astype(jnp.int32) == row_lanes, 1.0, 0.0).astype(BF)

    def slabs_of(buf, u):
        some = [buf[16 * z:16 * z + 16][4 * u:4 * u + 4] for z in range(2)]
        some = jnp.concatenate(some, axis=0).astype(F32)
        return some.reshape(NY, SH, KD).astype(BF)

    def xg1(u):
        xg[u, x] = slabs_of(got_x, u)
        for other in (xr, xl):
            send(xg.at[u, x], xg.at[u, x], s_xg1.at[u], m_xg1.at[u], at_x(other))

    def xg2(u):
        wait_for(m_xg1.at[u], xg.at[u, pl.ds(0, 2)])
        lower, upper = xg.at[u, xl, pl.ds(0, 2)], xg.at[u, xr, pl.ds(2, 2)]
        send(lower, lower, s_xg2.at[u], m_xg2.at[u], at_x(xr))
        send(upper, upper, s_xg2.at[u], m_xg2.at[u], at_x(xl))

    def add(*terms):
        total = terms[0].astype(F32)
        for term in terms[1:]:
            total = total + term.astype(F32)
        return total

    def forward_part(u):
        wait_for(m_xg2.at[u], xg.at[u, 0])
        for half in range(2):
            out = None
            for i in range(NX):
                term = dot_nn(xg[u, i].reshape(UR, KD), wx[i, half])
                out = term if out is None else out + term
            pf[u, :, :, FX * half:FX * half + FX] = out.astype(BF).reshape(NY, SH, FX)

    def f1(u):
        send(pf.at[u, y3], fb.at[u, 1], s_f1, m_f1.at[u], at_y(y1))
        send(pf.at[u, y1], fb.at[u, 0], s_f1, m_f1.at[u], at_y(y1))

    def f2(u):
        wait_for(m_f1.at[u], fb.at[u])
        pf[u, y2] = add(pf[u, y2], fb[u, 1]).astype(BF)
        send(pf.at[u, y2], fc.at[u], s_f2, m_f2.at[u], at_y(y2))

    def make_hidden(u):
        wait_for(m_f2.at[u], fc.at[u])
        total = add(pf[u, y], fb[u, 0], fc[u])
        gu_keep[u] = total
        gate, up = total[:, :FX], total[:, FX:]
        hid[u // 2, x, y, u % 2] = ((gate * jax.nn.sigmoid(gate)) * up).astype(BF)

    def backward_part(d):
        for uu in range(2):
            gs[d, :, uu] = slabs_of(got_g, 2 * d + uu)
        left = gs[d].reshape(2 * UR, KD)
        for i in range(NX):
            out = dot_nt(left, dn_ref[FX * i:FX * i + FX, :]).astype(BF)
            pv[d, i] = out.reshape(NY, 2, SH, FX)

    def x1(d):
        send(pv.at[d, xo, pl.ds(0, 2)], r1.at[d, 0], s_x1, m_x1.at[d], at_x(xr))
        send(pv.at[d, xo, pl.ds(2, 2)], r1.at[d, 1], s_x1, m_x1.at[d], at_x(xl))

    def x2_plain(d):
        send(pv.at[d, xr, pl.ds(2, 2)], r2.at[d, 0, pl.ds(2, 2)], s_x2, m_x2.at[d], at_x(xr))
        send(pv.at[d, xl, pl.ds(0, 2)], r2.at[d, 1, pl.ds(0, 2)], s_x2, m_x2.at[d], at_x(xl))

    def x2_added(d):
        wait_for(m_x1.at[d], r1.at[d])
        lower, upper = pl.ds(0, 2), pl.ds(2, 2)
        pv[d, xr, lower] = add(pv[d, xr, lower], r1[d, 0]).astype(BF)
        send(pv.at[d, xr, lower], r2.at[d, 0, lower], s_x2, m_x2.at[d], at_x(xr))
        pv[d, xl, upper] = add(pv[d, xl, upper], r1[d, 1]).astype(BF)
        send(pv.at[d, xl, upper], r2.at[d, 1, upper], s_x2, m_x2.at[d], at_x(xl))

    def v1(d):
        wait_for(m_x2.at[d], r2.at[d])
        qv[d] = add(pv[d, x], r2[d, 0], r2[d, 1]).astype(BF)
        send(qv.at[d, y3], vb.at[d, 1], s_v1, m_v1.at[d], at_y(y1))
        send(qv.at[d, y1], vb.at[d, 0], s_v1, m_v1.at[d], at_y(y1))

    def v2(d):
        wait_for(m_v1.at[d], vb.at[d])
        qv[d, y2] = add(qv[d, y2], vb[d, 1]).astype(BF)
        send(qv.at[d, y2], vc.at[d], s_v2, m_v2.at[d], at_y(y2))

    def make_act(d):
        wait_for(m_v2.at[d], vc.at[d])
        total = add(qv[d, y], vb[d, 0], vc[d])
        for uu in range(2):
            u = 2 * d + uu
            grad = total[uu]
            gate, up = gu_keep[u, :, :FX], gu_keep[u, :, FX:]
            sig = jax.nn.sigmoid(gate)
            act[u, x, y, :, :FX] = (grad * up * sig * (1.0 + gate * (1.0 - sig))).astype(BF)
            act[u, x, y, :, FX:] = (grad * (gate * sig)).astype(BF)

    def unit(a):
        return hid.at[a] if a < ND else act.at[a - ND]

    def ya1(a):
        block = unit(a).at[x, y]
        send(block, block, s_ya1.at[a], m_ya1.at[a], at_y(y2))
        send(block, block, s_ya2.at[a], m_ya2.at[a], at_y(y1))

    def ya2(a):
        block = unit(a).at[x, y2]
        wait_for(m_ya1.at[a], block)
        send(block, block, s_ya2.at[a], m_ya2.at[a], at_y(y1))

    def xa1(a):
        wait_for(m_ya2.at[a], unit(a).at[0, pl.ds(0, 2)])
        mine = unit(a).at[x]
        for other in (xr, xl):
            send(mine, mine, s_xa1.at[a], m_xa1.at[a], at_x(other))

    def xa2(a):
        wait_for(m_xa1.at[a], unit(a).at[pl.ds(0, 2)])
        lower, upper = unit(a).at[xl, pl.ds(0, 2)], unit(a).at[xr, pl.ds(2, 2)]
        send(lower, lower, s_xa2.at[a], m_xa2.at[a], at_x(xr))
        send(upper, upper, s_xa2.at[a], m_xa2.at[a], at_x(xl))

    def gathered(a):
        wait_for(m_xa2.at[a], unit(a).at[0])

    def send_unit(src, dst, u, n, rows_out):
        slabs = rows_out.reshape(8, CAP, KD).astype(BF)
        for z in range(2):
            src[16 * z + 4 * u:16 * z + 4 * u + 4] = slabs[4 * z:4 * z + 4]

        def one_peer(i, _):
            k = lax.rem(me + i, 8)
            peer = 16 * lax.div(k, 4) + 4 * u + lax.rem(k, 4)

            @pl.when(peer != me)
            def _():
                send(src.at[peer], dst.at[me], s_a2a.at[n], r_a2a.at[n], (dp, peer))

            return 0

        lax.fori_loop(0, 8, one_peer, 0)

    def use_hidden(d):
        gathered(d)
        out = None
        for i in range(NX):
            term = dot_nn(hid[d, i].reshape(2 * UR, FX), dn_ref[FX * i:FX * i + FX, :])
            out = term if out is None else out + term
        out = out.reshape(NY, 2, SH, KD)
        for uu in range(2):
            send_unit(send_o, got_o, 2 * d + uu, 2, out[:, uu].reshape(UR, KD))

    def hidden_weights(i):
        grads = dot_nn(gt[...], hid[:, i].reshape(ROWS, FX))
        dg_ref[FX * i:FX * i + FX, :] = grads.T.astype(BF)

    def use_act(u):
        gathered(ND + u)
        out = None
        for i in range(NX):
            for half in range(2):
                term = dot_nt(
                    act[u, i, :, :, FX * half:FX * half + FX].reshape(UR, FX),
                    w_ref[:, half * FF + FX * i:half * FF + FX * i + FX],
                )
                out = term if out is None else out + term
        send_unit(send_i, got_i, u, 3, out)

    def act_weights(d):
        for i in range(NX):
            for half in range(2):
                cols = slice(half * FF + FX * i, half * FF + FX * i + FX)
                right = act[2 * d:2 * d + 2, i, :, :, FX * half:FX * half + FX]
                grads = dot_nn(xt[d], right.reshape(2 * UR, FX))
                if d == 0:
                    gu_acc[:, cols] = grads
                else:
                    gu_ref[:, cols] = (gu_acc[:, cols] + grads).astype(BF)

    wait_for(r_a2a.at[0], got_x.at[pl.ds(0, NE - 1)])
    for u in range(NU):
        xg1(u)
    for copy in keep:
        copy.wait()
    wait_for(m_w, wx.at[pl.ds(0, NX - 1)])
    xg2(0)
    xg2(1)
    forward_part(0)
    f1(0)
    xg2(2)
    forward_part(1)
    f1(1)
    xg2(3)
    f2(0)
    fetch_dn.wait()
    wait_for(r_a2a.at[1], got_x.at[pl.ds(0, NE - 1)])
    backward_part(0)
    x1(0)
    x2_plain(0)
    forward_part(2)
    f1(2)
    f2(1)
    backward_part(1)
    x1(1)
    forward_part(3)
    f1(3)
    make_hidden(0)
    x2_added(0)
    x2_plain(1)
    make_hidden(1)
    ya1(0)
    f2(2)
    x2_added(1)
    f2(3)
    ya2(0)
    make_hidden(2)
    v1(0)
    make_hidden(3)
    ya1(1)
    xa1(0)
    v1(1)
    v2(0)
    ya2(1)
    v2(1)
    make_act(0)
    ya1(2)
    ya1(3)
    xa1(1)
    xa2(0)
    make_act(1)
    ya1(4)
    ya1(5)
    ya2(2)
    ya2(3)
    xa2(1)
    xa1(2)
    ya2(4)
    ya2(5)
    xa1(3)
    use_hidden(0)
    xa2(2)
    xa1(4)
    use_hidden(1)
    xa2(3)
    xa1(5)
    for d in range(ND):
        xt[d] = xg[2 * d:2 * d + 2, x].reshape(2 * UR, KD).T
    gt[...] = gs[...].reshape(ROWS, KD).T
    fetch_w.wait()
    use_act(0)
    xa2(4)
    for i in range(NX):
        hidden_weights(i)
    put_dg = pltpu.make_async_copy(dg_ref, dg_hbm, s_local.at[2])
    put_dg.start()
    use_act(1)
    xa2(5)
    act_weights(0)

    got_o[me] = send_o[me]
    back = arrived(got_o, 2)
    p0, p1 = dot_nn(hits[0], back), dot_nn(hits[1], back)
    lo_ref[...] = (gate0 * p0 + gate1 * p1).astype(BF)
    ones = jnp.ones((8, KD), F32)

    def lane_sums(values):
        return lax.dot_general(
            ones, values, (((1,), (1,)), ((), ())),
            precision=lax.Precision.HIGHEST, preferred_element_type=F32,
        )

    cot_again = cot_ref[...].astype(F32)
    first = lax.broadcasted_iota(jnp.int32, (8, TOK), 0) == 0
    gx[x] = jnp.where(first, lane_sums(cot_again * p0), lane_sums(cot_again * p1))
    for j, other in enumerate((xr, xo, xl)):
        send(gx.at[x], gx.at[x], s_gate.at[0, j], m_gate.at[0, x], at_x(other))
    use_act(2)
    for other in (xr, xo, xl):
        wait_for(m_gate.at[0, other], gx.at[other])
    gy[y] = (gx[0] + gx[1]) + (gx[2] + gx[3])
    for j in (1, 2, 3):
        send(gy.at[y], gy.at[y], s_gate.at[1, j - 1], m_gate.at[1, y], at_y(lax.rem(y + j, NY)))
    use_act(3)
    act_weights(1)
    put_gu = pltpu.make_async_copy(gu_ref, gu_hbm, s_local.at[3])
    put_gu.start()
    for j in (1, 2, 3):
        other = lax.rem(y + j, NY)
        wait_for(m_gate.at[1, other], gy.at[other])
    gg_ref[...] = ((gy[0] + gy[1]) + (gy[2] + gy[3]))[0:2]

    for n, buf in enumerate((send_x, send_g, send_o)):
        wait_for(s_a2a.at[n], buf.at[pl.ds(0, NE - 1)])
    wait_for(s_w, wx.at[pl.ds(0, NX - 1)])
    for u in range(NU):
        wait_for(s_xg1.at[u], xg.at[u, pl.ds(0, 2)])
        wait_for(s_xg2.at[u], xg.at[u, 0])
    wait_for(s_f1, fb)
    wait_for(s_f2, fc)
    wait_for(s_x1, r1)
    wait_for(s_x2, r2)
    wait_for(s_v1, vb)
    wait_for(s_v2, vc)
    for a in range(ND + NU):
        wait_for(s_ya1.at[a], unit(a).at[0, 0])
        wait_for(s_ya2.at[a], unit(a).at[0, pl.ds(0, 2)])
        wait_for(s_xa1.at[a], unit(a).at[pl.ds(0, 2)])
        wait_for(s_xa2.at[a], unit(a).at[0])
    for j in range(3):
        wait_for(s_gate.at[0, j], gx.at[0])
        wait_for(s_gate.at[1, j], gy.at[0])
    put_dg.wait()

    got_i[me] = send_i[me]
    back = arrived(got_i, 3)
    pair = dot_nn(hits[0], back) + dot_nn(hits[1], back)
    high = pair.astype(BF)
    low = (pair - high.astype(F32)).astype(BF)
    for b in range(KD // HB):
        cols = slice(b * HB, (b + 1) * HB)
        out = dot_nn(high[:, cols], signs[...]) + dot_nn(low[:, cols], signs[...])
        tg_ref[:, cols] = (out * (HB ** -0.5)).astype(BF)
    wait_for(s_a2a.at[3], send_x.at[pl.ds(0, NE - 1)])
    put_gu.wait()


def place_results(*refs):
    count = 5
    sources, targets, held = refs[:count], refs[count:2 * count], refs[2 * count:3 * count]
    s_in, s_out = refs[3 * count:]
    order = (3, 4, 0, 1, 2)
    fetch = {n: pltpu.make_async_copy(sources[n], held[n], s_in.at[n]) for n in order}
    put = {n: pltpu.make_async_copy(held[n], targets[n], s_out.at[n]) for n in order}
    for n in order:
        fetch[n].start()
    for n in order:
        fetch[n].wait()
        put[n].start()
    for n in order:
        put[n].wait()


def per_device(tokens, cotangent, expert_ids, gate_values, gate_up_weight, down_weight):
    vmem = pl.BlockSpec(memory_space=pltpu.VMEM)
    hbm = pl.BlockSpec(memory_space=pl.ANY)
    slabs = pltpu.VMEM((NE, CAP, KD), BF)
    dma = pltpu.SemaphoreType.DMA
    results = (
        jax.ShapeDtypeStruct((TOK, KD), BF),
        jax.ShapeDtypeStruct((TOK, KD), BF),
        jax.ShapeDtypeStruct((2, TOK), F32),
        jax.ShapeDtypeStruct((KD, 2 * FF), BF),
        jax.ShapeDtypeStruct((FF, KD), BF),
    )
    made = pl.pallas_call(
        kernel,
        out_shape=results,
        in_specs=[vmem] * 4 + [hbm] * 2,
        out_specs=[vmem] * 3 + [hbm] * 2,
        scratch_shapes=[
            pltpu.VMEM((KD, 2 * FF), BF), pltpu.VMEM((FF, KD), BF),
            pltpu.VMEM((KD, 2 * FF), BF), pltpu.VMEM((FF, KD), BF),
            pltpu.VMEM((KD, 2 * FF), F32), pltpu.VMEM((HB, HB), BF),
            pltpu.VMEM((NX, 2, KD, FX), BF),
            slabs, slabs, slabs, slabs, slabs, slabs, slabs, slabs,
            pltpu.VMEM((NU, NX, NY, SH, KD), BF),
            pltpu.VMEM((ND, NY, 2, SH, KD), BF),
            pltpu.VMEM((ND, KD, 2 * UR), BF), pltpu.VMEM((KD, ROWS), BF),
            pltpu.VMEM((2, TOK, ROWS), BF), pltpu.VMEM((2, ROWS, TOK), BF),
            pltpu.VMEM((NU, NY, SH, 2 * FX), BF),
            pltpu.VMEM((NU, 2, SH, 2 * FX), BF),
            pltpu.VMEM((NU, SH, 2 * FX), BF),
            pltpu.VMEM((ND, NX, NY, 2, SH, FX), BF),
            pltpu.VMEM((ND, 2, 2, 2, SH, FX), BF),
            pltpu.VMEM((ND, 2, NY, 2, SH, FX), BF),
            pltpu.VMEM((ND, NY, 2, SH, FX), BF),
            pltpu.VMEM((ND, 2, 2, SH, FX), BF),
            pltpu.VMEM((ND, 2, SH, FX), BF),
            pltpu.VMEM((NU, SH, 2 * FX), F32),
            pltpu.VMEM((ND, NX, NY, 2, SH, FX), BF),
            pltpu.VMEM((NU, NX, NY, SH, 2 * FX), BF),
            pltpu.VMEM((NX, 8, TOK), F32), pltpu.VMEM((NY, 8, TOK), F32),
            dma((6,)), dma((4,)), dma((4,)),
            dma, dma, dma((NU,)), dma((NU,)), dma((NU,)), dma((NU,)),
            dma, dma, dma((NU,)), dma((NU,)),
            dma, dma, dma((ND,)), dma((ND,)),
            dma, dma, dma((ND,)), dma((ND,)),
            dma((ND + NU,)), dma((ND + NU,)), dma((ND + NU,)), dma((ND + NU,)),
            dma((ND + NU,)), dma((ND + NU,)), dma((ND + NU,)), dma((ND + NU,)),
            dma((2, 3)), dma((2, 4)),
        ],
        compiler_params=pltpu.CompilerParams(
            collective_id=0, has_side_effects=True, vmem_limit_bytes=56 * 1024 * 1024
        ),
        cost_estimate=pl.CostEstimate(
            flops=2 * ROWS * KD * 9 * FF, bytes_accessed=6 * 1024 * 1024, transcendentals=ROWS * FF
        ),
    )(
        tokens, cotangent, expert_ids.T, gate_values.T, gate_up_weight[0], down_weight[0],
    )
    lo, tg, gg, gu, dg = pl.pallas_call(
        place_results,
        out_shape=results,
        in_specs=[hbm] * 5,
        out_specs=[hbm] * 5,
        scratch_shapes=[pltpu.VMEM(r.shape, r.dtype) for r in results] + [dma((5,)), dma((5,))],
    )(*made)
    return lo, tg, gg.T, gu[None], dg[None]


def solution(mesh):
    return jax.shard_map(
        per_device,
        mesh=mesh,
        in_specs=(
            P("expert", "dp"),
            P("expert", "dp"),
            P("expert", None),
            P("expert", None),
            P("expert", "dp", None),
            P("expert", None, "dp"),
        ),
        out_specs=(
            P("expert", "dp"),
            P("expert", "dp"),
            P("expert", None),
            P("expert", "dp", None),
            P("expert", None, "dp"),
        ),
        check_vma=False,
    )
```

```python
import functools

import jax
import jax.numpy as jnp
from jax import lax
from jax.experimental import pallas as pl
from jax.experimental.pallas import tpu as pltpu
from jax.sharding import PartitionSpec as P

HB = 128
MESH = pl.DeviceIdType.MESH
BF = jnp.bfloat16
F32 = jnp.float32

NX, NY = 4, 4
NE = 32
CAP = 24
ROWS = NE * CAP
TOK = 192
KD = 256
FF = 1024
FX = FF // NX
NU = 4
UR = ROWS // NU
SH = UR // NY
ND = 2
NEAR = ((0, 28), (4, 24), (12, 16), (8, 20))


def dot_nn(a, b):
    return lax.dot_general(a, b, (((1,), (0,)), ((), ())), preferred_element_type=F32)


def dot_nt(a, b):
    return lax.dot_general(a, b, (((1,), (1,)), ((), ())), preferred_element_type=F32)


def dot_tn(a, b):
    return lax.dot_general(a, b, (((0,), (0,)), ((), ())), preferred_element_type=F32)


def signs_of_block():
    common = jnp.bitwise_and(
        lax.broadcasted_iota(jnp.int32, (HB, HB), 0), lax.broadcasted_iota(jnp.int32, (HB, HB), 1)
    )
    for shift in (4, 2, 1):
        common = jnp.bitwise_xor(common, jnp.right_shift(common, shift))
    return (1 - 2 * jnp.bitwise_and(common, 1)).astype(F32).astype(BF)


def kernel(
    tok_ref, cot_ref, ids_ref, gate_ref, w_hbm, dn_hbm,
    lo_ref, tg_ref, gg_ref, gu_hbm, dg_hbm,
    w_ref, dn_ref, gu_ref, dg_ref, gu_acc, signs, wx,
    send_x, send_g, send_o, send_i, got_x, got_g, got_o, got_i,
    xg, gs, xt, gt, hits, hits_t,
    pf, fb, fc, pv, r1, r2, qv, vb, vc, gu_keep, hid, act, gx, gy,
    s_local, s_a2a, r_a2a, s_w, m_w, s_xg1, s_xg2, m_xg1, m_xg2,
    s_f1, s_f2, m_f1, m_f2, s_x1, s_x2, m_x1, m_x2, s_v1, s_v2, m_v1, m_v2,
    s_ya1, s_ya2, s_xa1, s_xa2, m_ya1, m_ya2, m_xa1, m_xa2, s_gate, m_gate,
):
    dp = lax.axis_index("dp")
    me = lax.axis_index("expert")
    x = lax.rem(dp, NX)
    y = lax.div(dp, NX)
    xr, xo, xl = lax.rem(x + 1, NX), lax.rem(x + 2, NX), lax.rem(x + 3, NX)
    y1, y2, y3 = y + 1 - 2 * lax.rem(y, 2), lax.rem(y + 2, NY), NY - 1 - y

    def at_x(other):
        return (y * NX + other, me)

    def at_y(other):
        return (other * NX + x, me)

    def send(src, dst, send_sem, recv_sem, device):
        pltpu.make_async_remote_copy(
            src_ref=src, dst_ref=dst, send_sem=send_sem, recv_sem=recv_sem,
            device_id=device, device_id_type=MESH,
        ).start()

    def wait_for(sem, ref):
        pltpu.make_async_copy(ref, ref, sem).wait()

    barrier = pltpu.get_barrier_semaphore()

    def greet(i, _):
        pl.semaphore_signal(
            barrier, inc=1, device_id=(dp, lax.rem(me + i, NE)), device_id_type=MESH
        )
        return 0

    lax.fori_loop(1, NE, greet, 0)
    for other in (xr, xo, xl):
        pl.semaphore_signal(barrier, inc=1, device_id=at_x(other), device_id_type=MESH)
    for j in (1, 2, 3):
        pl.semaphore_signal(
            barrier, inc=1, device_id=at_y(lax.rem(y + j, NY)), device_id_type=MESH
        )
    fetch_w = pltpu.make_async_copy(w_hbm, w_ref, s_local.at[0])
    fetch_dn = pltpu.make_async_copy(dn_hbm, dn_ref, s_local.at[1])
    fetch_w.start()
    fetch_dn.start()

    def own_columns(half, other):
        return w_hbm.at[:, pl.ds(pl.multiple_of(half * FF + FX * other, FX), FX)]

    keep = [
        pltpu.make_async_copy(own_columns(half, x), wx.at[x, half], s_local.at[4 + half])
        for half in range(2)
    ]
    for copy in keep:
        copy.start()

    places = lax.broadcasted_iota(jnp.int32, (NE, TOK), 0)
    one0 = jnp.where(ids_ref[0:1, :] == places, 1.0, 0.0)
    one1 = jnp.where(ids_ref[1:2, :] == places, 1.0, 0.0)
    before = jnp.where(
        lax.broadcasted_iota(jnp.int32, (TOK, TOK), 0)
        < lax.broadcasted_iota(jnp.int32, (TOK, TOK), 1),
        1.0, 0.0,
    ).astype(BF)
    earlier = dot_nn((one0 + one1).astype(BF), before)
    targets = []
    for k, one in enumerate((one0, one1)):
        rank = jnp.sum(one * earlier, axis=0, keepdims=True)
        targets.append(ids_ref[k:k + 1, :].astype(F32) * CAP + rank)
    rows = lax.broadcasted_iota(jnp.int32, (ROWS, TOK), 0)
    hit0 = targets[0].astype(jnp.int32) == rows
    hit1 = targets[1].astype(jnp.int32) == rows
    hits_t[0] = jnp.where(hit0, 1.0, 0.0).astype(BF)
    hits_t[1] = jnp.where(hit1, 1.0, 0.0).astype(BF)
    both = jnp.where(jnp.logical_or(hit0, hit1), 1.0, 0.0).astype(BF)

    pl.semaphore_wait(barrier, NE - 1 + 6)
    for half in range(2):
        for other in (xo, xr, xl):
            send(own_columns(half, other), wx.at[x, half], s_w, m_w, at_x(other))

    signs[...] = signs_of_block()
    pieces = []
    for b in range(KD // HB):
        block = dot_nn(tok_ref[:, b * HB:(b + 1) * HB], signs[...]) * (HB ** -0.5)
        top = jnp.max(jnp.abs(block), axis=1, keepdims=True) + 1e-06
        scale = jnp.broadcast_to(top, block.shape).astype(BF).astype(F32)
        coded = (block / scale).astype(BF)
        pieces.append((coded.astype(F32) * scale).astype(BF))
    restored = jnp.concatenate(pieces, axis=1)
    send_x[...] = dot_nn(both, restored).reshape(NE, CAP, KD).astype(BF)

    def scatter(src, dst, n):
        for u in range(NU):
            for base in NEAR[u]:

                def one_peer(i, _):
                    peer = lax.rem(me + i, NE)
                    send(src.at[peer], dst.at[i], s_a2a.at[n], r_a2a.at[n, u], (dp, peer))
                    return 0

                lax.fori_loop(max(base, 1), base + 4, one_peer, 0)
        dst[0] = src[me]

    def wait_unit(n, u):
        wait_for(r_a2a.at[n, u], got_x.at[pl.ds(0, 7 if u == 0 else 8)])

    def arrived(dst, n):
        wait_for(r_a2a.at[n, 0], got_x.at[pl.ds(0, NE - 1)])
        return dst[...].astype(F32).reshape(ROWS, KD).astype(BF)

    scatter(send_x, got_x, 0)

    small = jnp.concatenate(
        [targets[0], targets[1], gate_ref[...], jnp.zeros((4, TOK), F32)], axis=0
    )
    columns = jnp.concatenate([small, jnp.zeros((8, 256 - TOK), F32)], axis=1).T[:TOK]
    gate0, gate1 = columns[:, 2:3], columns[:, 3:4]
    cot = cot_ref[...].astype(F32)
    sent = dot_nn(hits_t[0], (gate0 * cot).astype(BF)) + dot_nn(hits_t[1], (gate1 * cot).astype(BF))
    send_g[...] = sent.reshape(NE, CAP, KD).astype(BF)
    scatter(send_g, got_g, 1)
    row_lanes = lax.broadcasted_iota(jnp.int32, (TOK, ROWS), 1)
    for k in range(2):
        hits[k] = jnp.where(columns[:, k:k + 1].astype(jnp.int32) == row_lanes, 1.0, 0.0).astype(BF)

    def slabs_of(buf, u):
        some = jnp.concatenate([buf[base:base + 4] for base in NEAR[u]], axis=0).astype(F32)
        return some.reshape(NY, SH, KD).astype(BF)

    def xg1(u):
        wait_unit(0, u)
        xg[u, x] = slabs_of(got_x, u)
        for other in (xr, xl):
            send(xg.at[u, x], xg.at[u, x], s_xg1.at[u], m_xg1.at[u], at_x(other))

    def xg2(u):
        wait_for(m_xg1.at[u], xg.at[u, pl.ds(0, 2)])
        lower, upper = xg.at[u, xl, pl.ds(0, 2)], xg.at[u, xr, pl.ds(2, 2)]
        send(lower, lower, s_xg2.at[u], m_xg2.at[u], at_x(xr))
        send(upper, upper, s_xg2.at[u], m_xg2.at[u], at_x(xl))

    def add(*terms):
        total = terms[0].astype(F32)
        for term in terms[1:]:
            total = total + term.astype(F32)
        return total

    def forward_part(u):
        wait_for(m_xg2.at[u], xg.at[u, 0])
        for half in range(2):
            out = None
            for i in range(NX):
                term = dot_nn(xg[u, i].reshape(UR, KD), wx[i, half])
                out = term if out is None else out + term
            pf[u, :, :, FX * half:FX * half + FX] = out.astype(BF).reshape(NY, SH, FX)

    def f1(u):
        send(pf.at[u, y3], fb.at[u, 1], s_f1, m_f1.at[u], at_y(y1))
        send(pf.at[u, y1], fb.at[u, 0], s_f1, m_f1.at[u], at_y(y1))

    def f2(u):
        wait_for(m_f1.at[u], fb.at[u])
        pf[u, y2] = add(pf[u, y2], fb[u, 1]).astype(BF)
        send(pf.at[u, y2], fc.at[u], s_f2, m_f2.at[u], at_y(y2))

    def make_hidden(u):
        wait_for(m_f2.at[u], fc.at[u])
        total = add(pf[u, y], fb[u, 0], fc[u])
        gu_keep[u] = total
        gate, up = total[:, :FX], total[:, FX:]
        hid[u // 2, x, y, u % 2] = ((gate * jax.nn.sigmoid(gate)) * up).astype(BF)

    def backward_part(d):
        for uu in range(2):
            wait_unit(1, 2 * d + uu)
            gs[d, :, uu] = slabs_of(got_g, 2 * d + uu)
        left = gs[d].reshape(2 * UR, KD)
        for i in range(NX):
            out = dot_nt(left, dn_ref[FX * i:FX * i + FX, :]).astype(BF)
            pv[d, i] = out.reshape(NY, 2, SH, FX)

    def x1(d):
        send(pv.at[d, xo, pl.ds(0, 2)], r1.at[d, 0], s_x1, m_x1.at[d], at_x(xr))
        send(pv.at[d, xo, pl.ds(2, 2)], r1.at[d, 1], s_x1, m_x1.at[d], at_x(xl))

    def x2_plain(d):
        send(pv.at[d, xr, pl.ds(2, 2)], r2.at[d, 0, pl.ds(2, 2)], s_x2, m_x2.at[d], at_x(xr))
        send(pv.at[d, xl, pl.ds(0, 2)], r2.at[d, 1, pl.ds(0, 2)], s_x2, m_x2.at[d], at_x(xl))

    def x2_added(d):
        wait_for(m_x1.at[d], r1.at[d])
        lower, upper = pl.ds(0, 2), pl.ds(2, 2)
        pv[d, xr, lower] = add(pv[d, xr, lower], r1[d, 0]).astype(BF)
        send(pv.at[d, xr, lower], r2.at[d, 0, lower], s_x2, m_x2.at[d], at_x(xr))
        pv[d, xl, upper] = add(pv[d, xl, upper], r1[d, 1]).astype(BF)
        send(pv.at[d, xl, upper], r2.at[d, 1, upper], s_x2, m_x2.at[d], at_x(xl))

    def v1(d):
        wait_for(m_x2.at[d], r2.at[d])
        qv[d] = add(pv[d, x], r2[d, 0], r2[d, 1]).astype(BF)
        send(qv.at[d, y3], vb.at[d, 1], s_v1, m_v1.at[d], at_y(y1))
        send(qv.at[d, y1], vb.at[d, 0], s_v1, m_v1.at[d], at_y(y1))

    def v2(d):
        wait_for(m_v1.at[d], vb.at[d])
        qv[d, y2] = add(qv[d, y2], vb[d, 1]).astype(BF)
        send(qv.at[d, y2], vc.at[d], s_v2, m_v2.at[d], at_y(y2))

    def make_act(d):
        wait_for(m_v2.at[d], vc.at[d])
        total = add(qv[d, y], vb[d, 0], vc[d])
        for uu in range(2):
            u = 2 * d + uu
            grad = total[uu]
            gate, up = gu_keep[u, :, :FX], gu_keep[u, :, FX:]
            sig = jax.nn.sigmoid(gate)
            act[u, x, y, :, :FX] = (grad * up * sig * (1.0 + gate * (1.0 - sig))).astype(BF)
            act[u, x, y, :, FX:] = (grad * (gate * sig)).astype(BF)

    def unit(a):
        return hid.at[a] if a < ND else act.at[a - ND]

    def ya1(a):
        block = unit(a).at[x, y]
        send(block, block, s_ya1.at[a], m_ya1.at[a], at_y(y2))
        send(block, block, s_ya2.at[a], m_ya2.at[a], at_y(y1))

    def ya2(a):
        block = unit(a).at[x, y2]
        wait_for(m_ya1.at[a], block)
        send(block, block, s_ya2.at[a], m_ya2.at[a], at_y(y1))

    def xa1(a):
        wait_for(m_ya2.at[a], unit(a).at[0, pl.ds(0, 2)])
        mine = unit(a).at[x]
        for other in (xr, xl):
            send(mine, mine, s_xa1.at[a], m_xa1.at[a], at_x(other))

    def xa2(a):
        wait_for(m_xa1.at[a], unit(a).at[pl.ds(0, 2)])
        lower, upper = unit(a).at[xl, pl.ds(0, 2)], unit(a).at[xr, pl.ds(2, 2)]
        send(lower, lower, s_xa2.at[a], m_xa2.at[a], at_x(xr))
        send(upper, upper, s_xa2.at[a], m_xa2.at[a], at_x(xl))

    def gathered(a):
        wait_for(m_xa2.at[a], unit(a).at[0])

    def send_unit(src, dst, u, n, rows_out):
        slabs = rows_out.reshape(8, CAP, KD).astype(BF)
        for z, base in enumerate(NEAR[u]):
            src[base:base + 4] = slabs[4 * z:4 * z + 4]

            def one_peer(i, _):
                peer = lax.rem(me + NE - i, NE)
                send(src.at[i], dst.at[me], s_a2a.at[n], r_a2a.at[n, 0], (dp, peer))
                return 0

            lax.fori_loop(max(base, 1), base + 4, one_peer, 0)

    def use_hidden(d):
        gathered(d)
        out = None
        for i in range(NX):
            term = dot_nn(hid[d, i].reshape(2 * UR, FX), dn_ref[FX * i:FX * i + FX, :])
            out = term if out is None else out + term
        out = out.reshape(NY, 2, SH, KD)
        for uu in range(2):
            send_unit(send_o, got_o, 2 * d + uu, 2, out[:, uu].reshape(UR, KD))

    def hidden_weights(i):
        grads = dot_nn(gt[...], hid[:, i].reshape(ROWS, FX))
        dg_ref[FX * i:FX * i + FX, :] = grads.T.astype(BF)

    def use_act(u):
        gathered(ND + u)
        out = None
        for i in range(NX):
            for half in range(2):
                term = dot_nt(
                    act[u, i, :, :, FX * half:FX * half + FX].reshape(UR, FX),
                    w_ref[:, half * FF + FX * i:half * FF + FX * i + FX],
                )
                out = term if out is None else out + term
        send_unit(send_i, got_i, u, 3, out)

    def act_weights(d):
        for i in range(NX):
            for half in range(2):
                cols = slice(half * FF + FX * i, half * FF + FX * i + FX)
                right = act[2 * d:2 * d + 2, i, :, :, FX * half:FX * half + FX]
                grads = dot_nn(xt[d], right.reshape(2 * UR, FX))
                if d == 0:
                    gu_acc[:, cols] = grads
                else:
                    gu_ref[:, cols] = (gu_acc[:, cols] + grads).astype(BF)

    def tokens_out():
        got_o[me] = send_o[0]
        back = arrived(got_o, 2)
        p0, p1 = dot_nn(hits[0], back), dot_nn(hits[1], back)
        lo_ref[...] = (gate0 * p0 + gate1 * p1).astype(BF)
        ones = jnp.ones((8, KD), F32)

        def lane_sums(values):
            return lax.dot_general(
                ones, values, (((1,), (1,)), ((), ())),
                precision=lax.Precision.HIGHEST, preferred_element_type=F32,
            )

        cot_again = cot_ref[...].astype(F32)
        first = lax.broadcasted_iota(jnp.int32, (8, TOK), 0) == 0
        gx[x] = jnp.where(first, lane_sums(cot_again * p0), lane_sums(cot_again * p1))
        for j, other in enumerate((xr, xo, xl)):
            send(gx.at[x], gx.at[x], s_gate.at[0, j], m_gate.at[0, x], at_x(other))

    def gate_pass():
        for other in (xr, xo, xl):
            wait_for(m_gate.at[0, other], gx.at[other])
        gy[y] = (gx[0] + gx[1]) + (gx[2] + gx[3])
        for j in (1, 2, 3):
            send(gy.at[y], gy.at[y], s_gate.at[1, j - 1], m_gate.at[1, y], at_y(lax.rem(y + j, NY)))

    xg1(0)
    xg1(1)
    xg2(0)
    xg1(3)
    xg2(1)
    for copy in keep:
        copy.wait()
    wait_for(m_w, wx.at[pl.ds(0, NX - 1)])
    forward_part(0)
    f1(0)
    xg2(3)
    xg1(2)
    forward_part(1)
    f1(1)
    f2(0)
    forward_part(3)
    f1(3)
    xg2(2)
    fetch_dn.wait()
    backward_part(0)
    x1(0)
    f2(1)
    forward_part(2)
    f1(2)
    x2_plain(0)
    f2(3)
    make_hidden(0)
    x2_added(0)
    make_hidden(1)
    ya1(0)
    backward_part(1)
    x1(1)
    f2(2)
    x2_plain(1)
    v1(0)
    make_hidden(3)
    ya2(0)
    x2_added(1)
    make_hidden(2)
    ya1(1)
    v2(0)
    xa1(0)
    ya2(1)
    v1(1)
    make_act(0)
    xa1(1)
    ya1(3)
    v2(1)
    ya1(2)
    xa2(0)
    for d in range(ND):
        xt[d] = xg[2 * d:2 * d + 2, x].reshape(2 * UR, KD).T
    gt[...] = gs[...].reshape(ROWS, KD).T
    ya2(3)
    xa2(1)
    make_act(1)
    xa1(3)
    ya2(2)
    ya1(4)
    xa1(2)
    ya1(5)
    ya2(4)
    use_hidden(1)
    xa2(3)
    xa1(4)
    ya2(5)
    xa2(2)
    fetch_w.wait()
    use_act(1)
    use_hidden(0)
    xa1(5)
    hidden_weights(0)
    hidden_weights(1)
    use_act(0)
    xa2(4)
    hidden_weights(2)
    hidden_weights(3)
    act_weights(0)
    xa2(5)
    use_act(2)
    use_act(3)
    tokens_out()
    put_dg = pltpu.make_async_copy(dg_ref, dg_hbm, s_local.at[2])
    put_dg.start()
    gate_pass()
    act_weights(1)
    put_gu = pltpu.make_async_copy(gu_ref, gu_hbm, s_local.at[3])
    put_gu.start()
    for j in (1, 2, 3):
        other = lax.rem(y + j, NY)
        wait_for(m_gate.at[1, other], gy.at[other])
    gg_ref[...] = ((gy[0] + gy[1]) + (gy[2] + gy[3]))[0:2]

    for n, buf in enumerate((send_x, send_g, send_o)):
        wait_for(s_a2a.at[n], buf.at[pl.ds(0, NE - 1)])
    wait_for(s_w, wx.at[pl.ds(0, NX - 1)])
    for u in range(NU):
        wait_for(s_xg1.at[u], xg.at[u, pl.ds(0, 2)])
        wait_for(s_xg2.at[u], xg.at[u, 0])
    wait_for(s_f1, fb)
    wait_for(s_f2, fc)
    wait_for(s_x1, r1)
    wait_for(s_x2, r2)
    wait_for(s_v1, vb)
    wait_for(s_v2, vc)
    for a in range(ND + NU):
        wait_for(s_ya1.at[a], unit(a).at[0, 0])
        wait_for(s_ya2.at[a], unit(a).at[0, pl.ds(0, 2)])
        wait_for(s_xa1.at[a], unit(a).at[pl.ds(0, 2)])
        wait_for(s_xa2.at[a], unit(a).at[0])
    for j in range(3):
        wait_for(s_gate.at[0, j], gx.at[0])
        wait_for(s_gate.at[1, j], gy.at[0])
    put_dg.wait()

    got_i[me] = send_i[0]
    back = arrived(got_i, 3)
    pair = dot_nn(hits[0], back) + dot_nn(hits[1], back)
    high = pair.astype(BF)
    low = (pair - high.astype(F32)).astype(BF)
    for b in range(KD // HB):
        cols = slice(b * HB, (b + 1) * HB)
        out = dot_nn(high[:, cols], signs[...]) + dot_nn(low[:, cols], signs[...])
        tg_ref[:, cols] = (out * (HB ** -0.5)).astype(BF)
    wait_for(s_a2a.at[3], send_x.at[pl.ds(0, NE - 1)])
    put_gu.wait()


def place_results(*refs):
    count = 5
    sources, targets, held = refs[:count], refs[count:2 * count], refs[2 * count:3 * count]
    s_in, s_out = refs[3 * count:]
    order = (3, 4, 0, 1, 2)
    fetch = {n: pltpu.make_async_copy(sources[n], held[n], s_in.at[n]) for n in order}
    put = {n: pltpu.make_async_copy(held[n], targets[n], s_out.at[n]) for n in order}
    for n in order:
        fetch[n].start()
    for n in order:
        fetch[n].wait()
        put[n].start()
    for n in order:
        put[n].wait()


def per_device(tokens, cotangent, expert_ids, gate_values, gate_up_weight, down_weight):
    vmem = pl.BlockSpec(memory_space=pltpu.VMEM)
    hbm = pl.BlockSpec(memory_space=pl.ANY)
    slabs = pltpu.VMEM((NE, CAP, KD), BF)
    dma = pltpu.SemaphoreType.DMA
    results = (
        jax.ShapeDtypeStruct((TOK, KD), BF),
        jax.ShapeDtypeStruct((TOK, KD), BF),
        jax.ShapeDtypeStruct((2, TOK), F32),
        jax.ShapeDtypeStruct((KD, 2 * FF), BF),
        jax.ShapeDtypeStruct((FF, KD), BF),
    )
    made = pl.pallas_call(
        kernel,
        out_shape=results,
        in_specs=[vmem] * 4 + [hbm] * 2,
        out_specs=[vmem] * 3 + [hbm] * 2,
        scratch_shapes=[
            pltpu.VMEM((KD, 2 * FF), BF), pltpu.VMEM((FF, KD), BF),
            pltpu.VMEM((KD, 2 * FF), BF), pltpu.VMEM((FF, KD), BF),
            pltpu.VMEM((KD, 2 * FF), F32), pltpu.VMEM((HB, HB), BF),
            pltpu.VMEM((NX, 2, KD, FX), BF),
            slabs, slabs, slabs, slabs, slabs, slabs, slabs, slabs,
            pltpu.VMEM((NU, NX, NY, SH, KD), BF),
            pltpu.VMEM((ND, NY, 2, SH, KD), BF),
            pltpu.VMEM((ND, KD, 2 * UR), BF), pltpu.VMEM((KD, ROWS), BF),
            pltpu.VMEM((2, TOK, ROWS), BF), pltpu.VMEM((2, ROWS, TOK), BF),
            pltpu.VMEM((NU, NY, SH, 2 * FX), BF),
            pltpu.VMEM((NU, 2, SH, 2 * FX), BF),
            pltpu.VMEM((NU, SH, 2 * FX), BF),
            pltpu.VMEM((ND, NX, NY, 2, SH, FX), BF),
            pltpu.VMEM((ND, 2, 2, 2, SH, FX), BF),
            pltpu.VMEM((ND, 2, NY, 2, SH, FX), BF),
            pltpu.VMEM((ND, NY, 2, SH, FX), BF),
            pltpu.VMEM((ND, 2, 2, SH, FX), BF),
            pltpu.VMEM((ND, 2, SH, FX), BF),
            pltpu.VMEM((NU, SH, 2 * FX), F32),
            pltpu.VMEM((ND, NX, NY, 2, SH, FX), BF),
            pltpu.VMEM((NU, NX, NY, SH, 2 * FX), BF),
            pltpu.VMEM((NX, 8, TOK), F32), pltpu.VMEM((NY, 8, TOK), F32),
            dma((6,)), dma((4,)), dma((4, NU)),
            dma, dma, dma((NU,)), dma((NU,)), dma((NU,)), dma((NU,)),
            dma, dma, dma((NU,)), dma((NU,)),
            dma, dma, dma((ND,)), dma((ND,)),
            dma, dma, dma((ND,)), dma((ND,)),
            dma((ND + NU,)), dma((ND + NU,)), dma((ND + NU,)), dma((ND + NU,)),
            dma((ND + NU,)), dma((ND + NU,)), dma((ND + NU,)), dma((ND + NU,)),
            dma((2, 3)), dma((2, 4)),
        ],
        compiler_params=pltpu.CompilerParams(
            collective_id=0, has_side_effects=True, vmem_limit_bytes=56 * 1024 * 1024
        ),
        cost_estimate=pl.CostEstimate(
            flops=2 * ROWS * KD * 9 * FF, bytes_accessed=6 * 1024 * 1024, transcendentals=ROWS * FF
        ),
    )(
        tokens, cotangent, expert_ids.T, gate_values.T, gate_up_weight[0], down_weight[0],
    )
    lo, tg, gg, gu, dg = pl.pallas_call(
        place_results,
        out_shape=results,
        in_specs=[hbm] * 5,
        out_specs=[hbm] * 5,
        scratch_shapes=[pltpu.VMEM(r.shape, r.dtype) for r in results] + [dma((5,)), dma((5,))],
    )(*made)
    return lo, tg, gg.T, gu[None], dg[None]


def solution(mesh):
    return jax.shard_map(
        per_device,
        mesh=mesh,
        in_specs=(
            P("expert", "dp"),
            P("expert", "dp"),
            P("expert", None),
            P("expert", None),
            P("expert", "dp", None),
            P("expert", None, "dp"),
        ),
        out_specs=(
            P("expert", "dp"),
            P("expert", "dp"),
            P("expert", None),
            P("expert", "dp", None),
            P("expert", None, "dp"),
        ),
        check_vma=False,
    )
```

```python
import functools

import jax
import jax.numpy as jnp
from jax import lax
from jax.experimental import pallas as pl
from jax.experimental.pallas import tpu as pltpu
from jax.sharding import PartitionSpec as P

HB = 128
MESH = pl.DeviceIdType.MESH
BF = jnp.bfloat16
F32 = jnp.float32

NX, NY = 4, 4
NE = 32
CAP = 24
ROWS = NE * CAP
TOK = 192
KD = 256
FF = 1024
FX = FF // NX
NU = 4
UR = ROWS // NU
SH = UR // NY
ND = 2
NEAR = ((0, 28), (4, 24), (12, 16), (8, 20))


def dot_nn(a, b):
    return lax.dot_general(a, b, (((1,), (0,)), ((), ())), preferred_element_type=F32)


def dot_nt(a, b):
    return lax.dot_general(a, b, (((1,), (1,)), ((), ())), preferred_element_type=F32)


def dot_tn(a, b):
    return lax.dot_general(a, b, (((0,), (0,)), ((), ())), preferred_element_type=F32)


def signs_of_block():
    common = jnp.bitwise_and(
        lax.broadcasted_iota(jnp.int32, (HB, HB), 0), lax.broadcasted_iota(jnp.int32, (HB, HB), 1)
    )
    for shift in (4, 2, 1):
        common = jnp.bitwise_xor(common, jnp.right_shift(common, shift))
    return (1 - 2 * jnp.bitwise_and(common, 1)).astype(F32).astype(BF)


def kernel(
    tok_ref, cot_ref, ids_ref, gate_ref, w_hbm, dn_hbm,
    lo_ref, tg_ref, gg_ref, gu_hbm, dg_hbm,
    w_ref, dn_ref, gu_ref, dg_ref, gu_acc, signs, wx,
    send_x, send_g, send_o, send_i, got_x, got_g, got_o, got_i,
    xg, gs, xt, gt, hits, hits_t,
    pf, fb, fc, pv, r1, r2, qv, vb, vc, gu_keep, hid, act, gx, gy,
    s_local, s_a2a, r_a2a, s_w, m_w, s_xg1, s_xg2, m_xg1, m_xg2,
    s_f1, s_f2, m_f1, m_f2, s_x1, s_x2, m_x1, m_x2, s_v1, s_v2, m_v1, m_v2,
    s_ya1, s_ya2, s_xa1, s_xa2, m_ya1, m_ya2, m_xa1, m_xa2, s_gate, m_gate,
):
    dp = lax.axis_index("dp")
    me = lax.axis_index("expert")
    x = lax.rem(dp, NX)
    y = lax.div(dp, NX)
    xr, xo, xl = lax.rem(x + 1, NX), lax.rem(x + 2, NX), lax.rem(x + 3, NX)
    y1, y2, y3 = y + 1 - 2 * lax.rem(y, 2), lax.rem(y + 2, NY), NY - 1 - y

    def at_x(other):
        return (y * NX + other, me)

    def at_y(other):
        return (other * NX + x, me)

    def send(src, dst, send_sem, recv_sem, device):
        pltpu.make_async_remote_copy(
            src_ref=src, dst_ref=dst, send_sem=send_sem, recv_sem=recv_sem,
            device_id=device, device_id_type=MESH,
        ).start()

    def wait_for(sem, ref):
        pltpu.make_async_copy(ref, ref, sem).wait()

    barrier = pltpu.get_barrier_semaphore()

    def greet(i, _):
        pl.semaphore_signal(
            barrier, inc=1, device_id=(dp, lax.rem(me + i, NE)), device_id_type=MESH
        )
        return 0

    lax.fori_loop(1, NE, greet, 0)
    for other in (xr, xo, xl):
        pl.semaphore_signal(barrier, inc=1, device_id=at_x(other), device_id_type=MESH)
    for j in (1, 2, 3):
        pl.semaphore_signal(
            barrier, inc=1, device_id=at_y(lax.rem(y + j, NY)), device_id_type=MESH
        )
    fetch_w = pltpu.make_async_copy(w_hbm, w_ref, s_local.at[0])
    fetch_dn = pltpu.make_async_copy(dn_hbm, dn_ref, s_local.at[1])
    fetch_w.start()
    fetch_dn.start()

    def own_columns(half, other):
        return w_hbm.at[:, pl.ds(pl.multiple_of(half * FF + FX * other, FX), FX)]

    keep = [
        pltpu.make_async_copy(own_columns(half, x), wx.at[x, half], s_local.at[4 + half])
        for half in range(2)
    ]
    for copy in keep:
        copy.start()

    places = lax.broadcasted_iota(jnp.int32, (NE, TOK), 0)
    one0 = jnp.where(ids_ref[0:1, :] == places, 1.0, 0.0)
    one1 = jnp.where(ids_ref[1:2, :] == places, 1.0, 0.0)
    before = jnp.where(
        lax.broadcasted_iota(jnp.int32, (TOK, TOK), 0)
        < lax.broadcasted_iota(jnp.int32, (TOK, TOK), 1),
        1.0, 0.0,
    ).astype(BF)
    earlier = dot_nn((one0 + one1).astype(BF), before)
    targets = []
    for k, one in enumerate((one0, one1)):
        rank = jnp.sum(one * earlier, axis=0, keepdims=True)
        targets.append(ids_ref[k:k + 1, :].astype(F32) * CAP + rank)
    rows = lax.broadcasted_iota(jnp.int32, (ROWS, TOK), 0)
    hit0 = targets[0].astype(jnp.int32) == rows
    hit1 = targets[1].astype(jnp.int32) == rows
    hits_t[0] = jnp.where(hit0, 1.0, 0.0).astype(BF)
    hits_t[1] = jnp.where(hit1, 1.0, 0.0).astype(BF)
    both = jnp.where(jnp.logical_or(hit0, hit1), 1.0, 0.0).astype(BF)

    pl.semaphore_wait(barrier, NE - 1 + 6)
    for half in range(2):
        for other in (xo, xr, xl):
            send(own_columns(half, other), wx.at[x, half], s_w, m_w, at_x(other))

    signs[...] = signs_of_block()
    pieces = []
    for b in range(KD // HB):
        block = dot_nn(tok_ref[:, b * HB:(b + 1) * HB], signs[...]) * (HB ** -0.5)
        top = jnp.max(jnp.abs(block), axis=1, keepdims=True) + 1e-06
        scale = jnp.broadcast_to(top, block.shape).astype(BF).astype(F32)
        coded = (block / scale).astype(BF)
        pieces.append((coded.astype(F32) * scale).astype(BF))
    restored = jnp.concatenate(pieces, axis=1)
    send_x[...] = dot_nn(both, restored).reshape(NE, CAP, KD).astype(BF)

    def scatter(src, dst, n):
        for u in range(NU):
            for base in NEAR[u]:

                def one_peer(i, _):
                    peer = lax.rem(me + i, NE)
                    send(src.at[peer], dst.at[i], s_a2a.at[n], r_a2a.at[n, u], (dp, peer))
                    return 0

                lax.fori_loop(max(base, 1), base + 4, one_peer, 0)
        dst[0] = src[me]

    def wait_unit(n, u):
        wait_for(r_a2a.at[n, u], got_x.at[pl.ds(0, 7 if u == 0 else 8)])

    def arrived(dst, n):
        wait_for(r_a2a.at[n, 0], got_x.at[pl.ds(0, NE - 1)])
        return dst[...].astype(F32).reshape(ROWS, KD).astype(BF)

    scatter(send_x, got_x, 0)

    small = jnp.concatenate(
        [targets[0], targets[1], gate_ref[...], jnp.zeros((4, TOK), F32)], axis=0
    )
    columns = jnp.concatenate([small, jnp.zeros((8, 256 - TOK), F32)], axis=1).T[:TOK]
    gate0, gate1 = columns[:, 2:3], columns[:, 3:4]
    cot = cot_ref[...].astype(F32)
    sent = dot_nn(hits_t[0], (gate0 * cot).astype(BF)) + dot_nn(hits_t[1], (gate1 * cot).astype(BF))
    send_g[...] = sent.reshape(NE, CAP, KD).astype(BF)
    scatter(send_g, got_g, 1)
    row_lanes = lax.broadcasted_iota(jnp.int32, (TOK, ROWS), 1)
    for k in range(2):
        hits[k] = jnp.where(columns[:, k:k + 1].astype(jnp.int32) == row_lanes, 1.0, 0.0).astype(BF)

    def slabs_of(buf, u):
        some = jnp.concatenate([buf[base:base + 4] for base in NEAR[u]], axis=0).astype(F32)
        return some.reshape(NY, SH, KD).astype(BF)

    def xg1(u):
        wait_unit(0, u)
        xg[u, x] = slabs_of(got_x, u)
        for other in (xr, xl):
            send(xg.at[u, x], xg.at[u, x], s_xg1.at[u], m_xg1.at[u], at_x(other))

    def xg2(u):
        wait_for(m_xg1.at[u], xg.at[u, pl.ds(0, 2)])
        lower, upper = xg.at[u, xl, pl.ds(0, 2)], xg.at[u, xr, pl.ds(2, 2)]
        send(lower, lower, s_xg2.at[u], m_xg2.at[u], at_x(xr))
        send(upper, upper, s_xg2.at[u], m_xg2.at[u], at_x(xl))

    def add(*terms):
        total = terms[0].astype(F32)
        for term in terms[1:]:
            total = total + term.astype(F32)
        return total

    def forward_part(u):
        wait_for(m_xg2.at[u], xg.at[u, 0])
        for half in range(2):
            out = None
            for i in range(NX):
                term = dot_nn(xg[u, i].reshape(UR, KD), wx[i, half])
                out = term if out is None else out + term
            pf[u, :, :, FX * half:FX * half + FX] = out.astype(BF).reshape(NY, SH, FX)

    def f1(u):
        send(pf.at[u, y3], fb.at[u, 1], s_f1, m_f1.at[u], at_y(y1))
        send(pf.at[u, y1], fb.at[u, 0], s_f1, m_f1.at[u], at_y(y1))

    def f2(u):
        wait_for(m_f1.at[u], fb.at[u])
        pf[u, y2] = add(pf[u, y2], fb[u, 1]).astype(BF)
        send(pf.at[u, y2], fc.at[u], s_f2, m_f2.at[u], at_y(y2))

    def make_hidden(u):
        wait_for(m_f2.at[u], fc.at[u])
        total = add(pf[u, y], fb[u, 0], fc[u])
        gu_keep[u] = total
        gate, up = total[:, :FX], total[:, FX:]
        hid[u // 2, x, y, u % 2] = ((gate * jax.nn.sigmoid(gate)) * up).astype(BF)

    def backward_part(d):
        for uu in range(2):
            wait_unit(1, 2 * d + uu)
            gs[d, :, uu] = slabs_of(got_g, 2 * d + uu)
        left = gs[d].reshape(2 * UR, KD)
        for i in range(NX):
            out = dot_nt(left, dn_ref[FX * i:FX * i + FX, :]).astype(BF)
            pv[d, i] = out.reshape(NY, 2, SH, FX)

    def x1(d):
        send(pv.at[d, xo, pl.ds(0, 2)], r1.at[d, 0], s_x1, m_x1.at[d], at_x(xr))
        send(pv.at[d, xo, pl.ds(2, 2)], r1.at[d, 1], s_x1, m_x1.at[d], at_x(xl))

    def x2_plain(d):
        send(pv.at[d, xr, pl.ds(2, 2)], r2.at[d, 0, pl.ds(2, 2)], s_x2, m_x2.at[d], at_x(xr))
        send(pv.at[d, xl, pl.ds(0, 2)], r2.at[d, 1, pl.ds(0, 2)], s_x2, m_x2.at[d], at_x(xl))

    def x2_added(d):
        wait_for(m_x1.at[d], r1.at[d])
        lower, upper = pl.ds(0, 2), pl.ds(2, 2)
        pv[d, xr, lower] = add(pv[d, xr, lower], r1[d, 0]).astype(BF)
        send(pv.at[d, xr, lower], r2.at[d, 0, lower], s_x2, m_x2.at[d], at_x(xr))
        pv[d, xl, upper] = add(pv[d, xl, upper], r1[d, 1]).astype(BF)
        send(pv.at[d, xl, upper], r2.at[d, 1, upper], s_x2, m_x2.at[d], at_x(xl))

    def v1(d):
        wait_for(m_x2.at[d], r2.at[d])
        qv[d] = add(pv[d, x], r2[d, 0], r2[d, 1]).astype(BF)
        send(qv.at[d, y3], vb.at[d, 1], s_v1, m_v1.at[d], at_y(y1))
        send(qv.at[d, y1], vb.at[d, 0], s_v1, m_v1.at[d], at_y(y1))

    def v2(d):
        wait_for(m_v1.at[d], vb.at[d])
        qv[d, y2] = add(qv[d, y2], vb[d, 1]).astype(BF)
        send(qv.at[d, y2], vc.at[d], s_v2, m_v2.at[d], at_y(y2))

    def make_act(d):
        wait_for(m_v2.at[d], vc.at[d])
        total = add(qv[d, y], vb[d, 0], vc[d])
        for uu in range(2):
            u = 2 * d + uu
            grad = total[uu]
            gate, up = gu_keep[u, :, :FX], gu_keep[u, :, FX:]
            sig = jax.nn.sigmoid(gate)
            act[u, x, y, :, :FX] = (grad * up * sig * (1.0 + gate * (1.0 - sig))).astype(BF)
            act[u, x, y, :, FX:] = (grad * (gate * sig)).astype(BF)

    def unit(a):
        return hid.at[a] if a < ND else act.at[a - ND]

    def ya1(a):
        block = unit(a).at[x, y]
        send(block, block, s_ya1.at[a], m_ya1.at[a], at_y(y2))
        send(block, block, s_ya2.at[a], m_ya2.at[a], at_y(y1))

    def ya2(a):
        block = unit(a).at[x, y2]
        wait_for(m_ya1.at[a], block)
        send(block, block, s_ya2.at[a], m_ya2.at[a], at_y(y1))

    def xa1(a):
        wait_for(m_ya2.at[a], unit(a).at[0, pl.ds(0, 2)])
        mine = unit(a).at[x]
        for other in (xr, xl):
            send(mine, mine, s_xa1.at[a], m_xa1.at[a], at_x(other))

    def xa2(a):
        wait_for(m_xa1.at[a], unit(a).at[pl.ds(0, 2)])
        lower, upper = unit(a).at[xl, pl.ds(0, 2)], unit(a).at[xr, pl.ds(2, 2)]
        send(lower, lower, s_xa2.at[a], m_xa2.at[a], at_x(xr))
        send(upper, upper, s_xa2.at[a], m_xa2.at[a], at_x(xl))

    def gathered(a):
        wait_for(m_xa2.at[a], unit(a).at[0])

    def send_unit(src, dst, u, n, rows_out):
        slabs = rows_out.reshape(8, CAP, KD).astype(BF)
        for z, base in enumerate(NEAR[u]):
            src[base:base + 4] = slabs[4 * z:4 * z + 4]

            def one_peer(i, _):
                peer = lax.rem(me + NE - i, NE)
                send(src.at[i], dst.at[me], s_a2a.at[n], r_a2a.at[n, 0], (dp, peer))
                return 0

            lax.fori_loop(max(base, 1), base + 4, one_peer, 0)

    def use_hidden(d):
        gathered(d)
        out = None
        for i in range(NX):
            term = dot_nn(hid[d, i].reshape(2 * UR, FX), dn_ref[FX * i:FX * i + FX, :])
            out = term if out is None else out + term
        out = out.reshape(NY, 2, SH, KD)
        for uu in range(2):
            send_unit(send_o, got_o, 2 * d + uu, 2, out[:, uu].reshape(UR, KD))

    def hidden_weights(i):
        grads = dot_nn(gt[...], hid[:, i].reshape(ROWS, FX))
        dg_ref[FX * i:FX * i + FX, :] = grads.T.astype(BF)

    def use_act(u):
        gathered(ND + u)
        out = None
        for i in range(NX):
            for half in range(2):
                term = dot_nt(
                    act[u, i, :, :, FX * half:FX * half + FX].reshape(UR, FX),
                    w_ref[:, half * FF + FX * i:half * FF + FX * i + FX],
                )
                out = term if out is None else out + term
        send_unit(send_i, got_i, u, 3, out)

    def act_weights(d):
        for i in range(NX):
            for half in range(2):
                cols = slice(half * FF + FX * i, half * FF + FX * i + FX)
                right = act[2 * d:2 * d + 2, i, :, :, FX * half:FX * half + FX]
                grads = dot_nn(xt[d], right.reshape(2 * UR, FX))
                if d == 0:
                    gu_acc[:, cols] = grads
                else:
                    gu_ref[:, cols] = (gu_acc[:, cols] + grads).astype(BF)

    def tokens_out():
        got_o[me] = send_o[0]
        back = arrived(got_o, 2)
        p0, p1 = dot_nn(hits[0], back), dot_nn(hits[1], back)
        lo_ref[...] = (gate0 * p0 + gate1 * p1).astype(BF)
        ones = jnp.ones((8, KD), F32)

        def lane_sums(values):
            return lax.dot_general(
                ones, values, (((1,), (1,)), ((), ())),
                precision=lax.Precision.HIGHEST, preferred_element_type=F32,
            )

        cot_again = cot_ref[...].astype(F32)
        first = lax.broadcasted_iota(jnp.int32, (8, TOK), 0) == 0
        gx[x] = jnp.where(first, lane_sums(cot_again * p0), lane_sums(cot_again * p1))
        for j, other in enumerate((xr, xo, xl)):
            send(gx.at[x], gx.at[x], s_gate.at[0, j], m_gate.at[0, x], at_x(other))

    def gate_pass():
        for other in (xr, xo, xl):
            wait_for(m_gate.at[0, other], gx.at[other])
        gy[y] = (gx[0] + gx[1]) + (gx[2] + gx[3])
        for j in (1, 2, 3):
            send(gy.at[y], gy.at[y], s_gate.at[1, j - 1], m_gate.at[1, y], at_y(lax.rem(y + j, NY)))

    xg1(0)
    xg1(1)
    xg2(0)
    xg1(3)
    xg2(1)
    for copy in keep:
        copy.wait()
    wait_for(m_w, wx.at[pl.ds(0, NX - 1)])
    forward_part(0)
    f1(0)
    xg2(3)
    xg1(2)
    forward_part(1)
    f1(1)
    f2(0)
    forward_part(3)
    f1(3)
    xg2(2)
    fetch_dn.wait()
    backward_part(0)
    x1(0)
    f2(1)
    forward_part(2)
    f1(2)
    x2_plain(0)
    f2(3)
    make_hidden(0)
    x2_added(0)
    make_hidden(1)
    ya1(0)
    backward_part(1)
    x1(1)
    f2(2)
    x2_plain(1)
    v1(0)
    make_hidden(3)
    ya2(0)
    x2_added(1)
    make_hidden(2)
    ya1(1)
    v2(0)
    xa1(0)
    ya2(1)
    v1(1)
    make_act(0)
    xa1(1)
    ya1(3)
    v2(1)
    ya1(2)
    xa2(0)
    for d in range(ND):
        xt[d] = xg[2 * d:2 * d + 2, x].reshape(2 * UR, KD).T
    gt[...] = gs[...].reshape(ROWS, KD).T
    ya2(3)
    xa2(1)
    make_act(1)
    xa1(3)
    ya2(2)
    ya1(4)
    xa1(2)
    ya1(5)
    ya2(4)
    use_hidden(1)
    xa2(3)
    xa1(4)
    ya2(5)
    xa2(2)
    fetch_w.wait()
    use_act(1)
    use_hidden(0)
    xa1(5)
    hidden_weights(0)
    hidden_weights(1)
    use_act(0)
    xa2(4)
    hidden_weights(2)
    hidden_weights(3)
    act_weights(0)
    xa2(5)
    use_act(2)
    use_act(3)
    tokens_out()
    put_dg = pltpu.make_async_copy(dg_ref, dg_hbm, s_local.at[2])
    put_dg.start()
    gate_pass()
    act_weights(1)
    put_gu = pltpu.make_async_copy(gu_ref, gu_hbm, s_local.at[3])
    put_gu.start()
    for j in (1, 2, 3):
        other = lax.rem(y + j, NY)
        wait_for(m_gate.at[1, other], gy.at[other])
    gg_ref[...] = ((gy[0] + gy[1]) + (gy[2] + gy[3]))[0:2]

    for n, buf in enumerate((send_x, send_g, send_o)):
        wait_for(s_a2a.at[n], buf.at[pl.ds(0, NE - 1)])
    wait_for(s_w, wx.at[pl.ds(0, NX - 1)])
    for u in range(NU):
        wait_for(s_xg1.at[u], xg.at[u, pl.ds(0, 2)])
        wait_for(s_xg2.at[u], xg.at[u, 0])
    wait_for(s_f1, fb)
    wait_for(s_f2, fc)
    wait_for(s_x1, r1)
    wait_for(s_x2, r2)
    wait_for(s_v1, vb)
    wait_for(s_v2, vc)
    for a in range(ND + NU):
        wait_for(s_ya1.at[a], unit(a).at[0, 0])
        wait_for(s_ya2.at[a], unit(a).at[0, pl.ds(0, 2)])
        wait_for(s_xa1.at[a], unit(a).at[pl.ds(0, 2)])
        wait_for(s_xa2.at[a], unit(a).at[0])
    for j in range(3):
        wait_for(s_gate.at[0, j], gx.at[0])
        wait_for(s_gate.at[1, j], gy.at[0])
    put_dg.wait()

    got_i[me] = send_i[0]
    back = arrived(got_i, 3)
    pair = dot_nn(hits[0], back) + dot_nn(hits[1], back)
    high = pair.astype(BF)
    low = (pair - high.astype(F32)).astype(BF)
    for b in range(KD // HB):
        cols = slice(b * HB, (b + 1) * HB)
        out = dot_nn(high[:, cols], signs[...]) + dot_nn(low[:, cols], signs[...])
        tg_ref[:, cols] = (out * (HB ** -0.5)).astype(BF)
    wait_for(s_a2a.at[3], send_x.at[pl.ds(0, NE - 1)])
    put_gu.wait()


PIECES = tuple((3, r, 64) for r in range(0, KD, 64)) + tuple((4, r, 256) for r in range(0, FF, 256)) + (
    (0, 0, TOK), (1, 0, TOK), (2, 0, 2)
)


def place_results(*refs):
    count = 5
    sources, targets, held = refs[:count], refs[count:2 * count], refs[2 * count:3 * count]
    s_in, s_out = refs[3 * count:]
    fetch, put = [], []
    for k, (n, row, size) in enumerate(PIECES):
        rows = pl.ds(row, size)
        fetch.append(pltpu.make_async_copy(sources[n].at[rows], held[n].at[rows], s_in.at[k]))
        put.append(pltpu.make_async_copy(held[n].at[rows], targets[n].at[rows], s_out.at[k]))
    for copy in fetch:
        copy.start()
    for k in range(len(PIECES)):
        fetch[k].wait()
        put[k].start()
    for copy in put:
        copy.wait()


def per_device(tokens, cotangent, expert_ids, gate_values, gate_up_weight, down_weight):
    vmem = pl.BlockSpec(memory_space=pltpu.VMEM)
    hbm = pl.BlockSpec(memory_space=pl.ANY)
    slabs = pltpu.VMEM((NE, CAP, KD), BF)
    dma = pltpu.SemaphoreType.DMA
    results = (
        jax.ShapeDtypeStruct((TOK, KD), BF),
        jax.ShapeDtypeStruct((TOK, KD), BF),
        jax.ShapeDtypeStruct((2, TOK), F32),
        jax.ShapeDtypeStruct((KD, 2 * FF), BF),
        jax.ShapeDtypeStruct((FF, KD), BF),
    )
    made = pl.pallas_call(
        kernel,
        out_shape=results,
        in_specs=[vmem] * 4 + [hbm] * 2,
        out_specs=[vmem] * 3 + [hbm] * 2,
        scratch_shapes=[
            pltpu.VMEM((KD, 2 * FF), BF), pltpu.VMEM((FF, KD), BF),
            pltpu.VMEM((KD, 2 * FF), BF), pltpu.VMEM((FF, KD), BF),
            pltpu.VMEM((KD, 2 * FF), F32), pltpu.VMEM((HB, HB), BF),
            pltpu.VMEM((NX, 2, KD, FX), BF),
            slabs, slabs, slabs, slabs, slabs, slabs, slabs, slabs,
            pltpu.VMEM((NU, NX, NY, SH, KD), BF),
            pltpu.VMEM((ND, NY, 2, SH, KD), BF),
            pltpu.VMEM((ND, KD, 2 * UR), BF), pltpu.VMEM((KD, ROWS), BF),
            pltpu.VMEM((2, TOK, ROWS), BF), pltpu.VMEM((2, ROWS, TOK), BF),
            pltpu.VMEM((NU, NY, SH, 2 * FX), BF),
            pltpu.VMEM((NU, 2, SH, 2 * FX), BF),
            pltpu.VMEM((NU, SH, 2 * FX), BF),
            pltpu.VMEM((ND, NX, NY, 2, SH, FX), BF),
            pltpu.VMEM((ND, 2, 2, 2, SH, FX), BF),
            pltpu.VMEM((ND, 2, NY, 2, SH, FX), BF),
            pltpu.VMEM((ND, NY, 2, SH, FX), BF),
            pltpu.VMEM((ND, 2, 2, SH, FX), BF),
            pltpu.VMEM((ND, 2, SH, FX), BF),
            pltpu.VMEM((NU, SH, 2 * FX), F32),
            pltpu.VMEM((ND, NX, NY, 2, SH, FX), BF),
            pltpu.VMEM((NU, NX, NY, SH, 2 * FX), BF),
            pltpu.VMEM((NX, 8, TOK), F32), pltpu.VMEM((NY, 8, TOK), F32),
            dma((6,)), dma((4,)), dma((4, NU)),
            dma, dma, dma((NU,)), dma((NU,)), dma((NU,)), dma((NU,)),
            dma, dma, dma((NU,)), dma((NU,)),
            dma, dma, dma((ND,)), dma((ND,)),
            dma, dma, dma((ND,)), dma((ND,)),
            dma((ND + NU,)), dma((ND + NU,)), dma((ND + NU,)), dma((ND + NU,)),
            dma((ND + NU,)), dma((ND + NU,)), dma((ND + NU,)), dma((ND + NU,)),
            dma((2, 3)), dma((2, 4)),
        ],
        compiler_params=pltpu.CompilerParams(
            collective_id=0, has_side_effects=True, vmem_limit_bytes=56 * 1024 * 1024
        ),
        cost_estimate=pl.CostEstimate(
            flops=2 * ROWS * KD * 9 * FF, bytes_accessed=6 * 1024 * 1024, transcendentals=ROWS * FF
        ),
    )(
        tokens, cotangent, expert_ids.T, gate_values.T, gate_up_weight[0], down_weight[0],
    )
    lo, tg, gg, gu, dg = pl.pallas_call(
        place_results,
        out_shape=results,
        in_specs=[hbm] * 5,
        out_specs=[hbm] * 5,
        scratch_shapes=[pltpu.VMEM(r.shape, r.dtype) for r in results] + [dma((len(PIECES),)), dma((len(PIECES),))],
    )(*made)
    return lo, tg, gg.T, gu[None], dg[None]


def solution(mesh):
    return jax.shard_map(
        per_device,
        mesh=mesh,
        in_specs=(
            P("expert", "dp"),
            P("expert", "dp"),
            P("expert", None),
            P("expert", None),
            P("expert", "dp", None),
            P("expert", None, "dp"),
        ),
        out_specs=(
            P("expert", "dp"),
            P("expert", "dp"),
            P("expert", None),
            P("expert", "dp", None),
            P("expert", None, "dp"),
        ),
        check_vma=False,
    )
```
